128 devices in a mesh: section: 32 (over z, y, core), tensor: 2 (over x_lo), dp: 2 (over x_hi).
Axes of the slice: x: 4 (x_hi: 2, x_lo: 2; x = x_hi * 2 + x_lo), y: 4, z: 4, core: 2. Of those that a mesh axis runs over, the one named last changes fastest.
Arguments:
- src_in: bfloat16 [8192, 768], P(('section', 'dp')), may hold values from -6 to 6
- tgt_in: bfloat16 [8192, 768], P(('section', 'dp')), may hold values from -6 to 6
- src_seg: int32 [8192], replicated, may hold values from 0 to 3, as said below
- tgt_seg: int32 [8192], replicated, may hold values from 0 to 3, as said below
- attn_in: bfloat16 [3, 3, 768, 768], P(None, None, 'section', 'tensor'), may hold values from -0.21875 to 0.21875
- attn_out: bfloat16 [3, 768, 768], P(None, 'tensor', 'section'), may hold values from -0.875 to 0.875
- w_up: bfloat16 [2, 768, 3072], P(None, 'section', 'tensor'), may hold values from -0.21875 to 0.21875
- w_down: bfloat16 [2, 3072, 768], P(None, 'tensor', 'section'), may hold values from -0.109375 to 0.109375
- qv_bias: bfloat16 [3, 2, 12, 64], P(None, None, 'tensor', 'section'), may hold values from -3 to 3
- up_bias: bfloat16 [2, 48, 64], P(None, 'tensor', 'section'), may hold values from -3 to 3
- gains: bfloat16 [5, 768], P(None, 'section'), may hold values from 0.5 to 1.5
- shifts: bfloat16 [10, 768], P(None, 'section'), may hold values from -3 to 3
- d_out: bfloat16 [8192, 768], P(('section', 'dp')), may hold values from -6 to 6
Outputs:
- dec_out: bfloat16 [8192, 768], P(('section', 'dp'))
- grad_src: float32 [8192, 768], P(('section', 'dp'))
- grad_tgt: float32 [8192, 768], P(('section', 'dp'))
- grad_attn_in: float32 [3, 3, 768, 768], P(None, None, 'section', 'tensor')
- grad_attn_out: float32 [3, 768, 768], P(None, 'tensor', 'section')
- grad_w_up: float32 [2, 768, 3072], P(None, 'section', 'tensor')
- grad_w_down: float32 [2, 3072, 768], P(None, 'tensor', 'section')
- grad_qv_bias: float32 [3, 2, 12, 64], P(None, None, 'tensor', 'section')
- grad_up_bias: float32 [2, 48, 64], P(None, 'tensor', 'section')
- grad_gains: float32 [5, 768], P(None, 'section')
- grad_shifts: float32 [10, 768], P(None, 'section')
The draws below stay inside these ranges and needn't reach their ends.
Inputs may be any that keep to these rules, and one draw needn't show every extreme that they name: `src_seg`: in each block of 128 positions the numbers start at 0 and never fall. Block j holds only 0 where j // 2 is odd, and 0, 1, 2 and 3, each at least once, where it is even. `tgt_seg`: same law as src_seg, with the parity reversed: block j holds only 0 where j // 2 is even; lengths drawn independently.
All inputs are finite; a program needn't handle non-finite values.
Results may differ from the reference program's by a relative error of at most 0.035.
Values may be sent and summed in bfloat16 or wider, within the bound.
A program may use at most 192 MiB of HBM per device.

```python
from functools import partial
import jax
import jax.numpy as jnp
from jax import lax

D = 768
HEADS = 12
HEAD_DIM = 64
FF = 3072
TOK_DEV = 128
REPLICAS = 2
TOKENS = 8192
N_SECTION = 32


def segment_layout(key, flip):
    blocks = TOKENS // TOK_DEV
    keys = jax.random.split(key, blocks)

    def one_block(block_key):
        cuts = jnp.sort(jax.random.permutation(block_key, TOK_DEV - 1)[:3] + 1)
        local = jnp.arange(TOK_DEV, dtype=jnp.int32)
        return jnp.sum((local[:, None] >= cuts[None, :]).astype(jnp.int32), axis=1).astype(jnp.int32)
    four = jax.vmap(one_block)(keys)
    section_of = jnp.arange(blocks, dtype=jnp.int32) // REPLICAS
    single = (section_of + flip) % 2 == 0
    return jnp.where(single[:, None], jnp.zeros_like(four), four).reshape(-1).astype(jnp.int32)


def draw_src_seg(key, part):
    key = jax.random.fold_in(key, 11)
    return segment_layout(key, 1)


def draw_tgt_seg(key, part):
    key = jax.random.fold_in(key, 23)
    return segment_layout(key, 0)


def level_of(stream_key, dims, cuts, smallest, largest):
    level = 1.0
    for position, blocks in cuts:
        heights = jax.random.uniform(jax.random.fold_in(jax.random.fold_in(stream_key, 6), position), (blocks,), jnp.float32, smallest / len(cuts), largest / len(cuts))
        level = level * jnp.repeat(jnp.exp(heights), dims[position] // blocks).reshape((-1,) + (1,) * (len(dims) - 1 - position))
    return level


def gaussian(stream_key, shape, scale, reach, cuts=(), kind=jnp.bfloat16):
    factor_of = level_of(stream_key, shape, cuts, -0.22, 0.18) if cuts else 1.0
    array = jax.random.normal(stream_key, shape, jnp.float32) * scale * factor_of
    return jnp.minimum(jnp.maximum(array, -reach), reach).astype(kind)


def setup_inputs(seed: int = 0) -> dict:
    splits = jax.random.split(jax.random.key(seed), 14)
    src_in = gaussian(splits[0], (TOKENS, D), 1.0, 6.0, ((0, 64),))
    tgt_in = gaussian(splits[1], (TOKENS, D), 1.0, 6.0, ((0, 64),))
    src_seg = draw_src_seg(jax.random.fold_in(splits[13], 71), 0)
    tgt_seg = draw_tgt_seg(jax.random.fold_in(splits[13], 71), 0)
    attn_in = gaussian(splits[4], (3, 3, D, D), D ** -0.5, 0.21875, ((2, 32), (3, 2)))
    attn_out = gaussian(splits[5], (3, D, D), (D // 16) ** -0.5, 0.875, ((1, 2), (2, 32)))
    w_up = gaussian(splits[6], (2, D, FF), D ** -0.5, 0.21875, ((1, 32), (2, 2)))
    w_down = gaussian(splits[7], (2, FF, D), FF ** -0.5, 0.109375, ((1, 2), (2, 32)))
    qv_bias = gaussian(splits[8], (3, 2, HEADS, HEAD_DIM), 0.5, 3.0, ((2, 2), (3, 32)))
    up_bias = gaussian(splits[9], (2, FF // HEAD_DIM, HEAD_DIM), 0.5, 3.0, ((1, 2), (2, 32)))
    gains = jnp.clip(1.0 + 0.1 * jax.random.normal(splits[10], (5, D), jnp.float32), 0.5, 1.5).astype(jnp.bfloat16)
    shifts = gaussian(splits[11], (10, D), 0.5, 3.0, ((1, 32),))
    d_out = gaussian(splits[12], (TOKENS, D), 1.0, 6.0, ((0, 64),))
    return dict(src_in=src_in, tgt_in=tgt_in, src_seg=src_seg, tgt_seg=tgt_seg, attn_in=attn_in, attn_out=attn_out, w_up=w_up, w_down=w_down, qv_bias=qv_bias, up_bias=up_bias, gains=gains, shifts=shifts, d_out=d_out)


@jax.custom_vjp
def low(v):
    return lax.optimization_barrier(v.astype(jnp.bfloat16)).astype(jnp.float32)

@jax.custom_vjp
def low_back(v):
    return v

def low_keep(v):
    return (low(v), None)

def low_pass(kept, grad):
    return (grad,)

def back_keep(v):
    return (v, None)

def back_low(kept, grad):
    return (low(grad),)
low.defvjp(low_keep, low_pass)
low_back.defvjp(back_keep, back_low)

def matmul(left, right):
    return jnp.dot(left, right, precision=lax.Precision.HIGHEST)

def layer_norm(resid, gain, shift):
    center = resid - lax.optimization_barrier(jnp.mean(resid, axis=-1, keepdims=True))
    spread = lax.optimization_barrier(jnp.mean(center * center, axis=-1, keepdims=True))
    return center * lax.rsqrt(spread + 1e-05) * gain + shift

def paired(values):
    shaped = values.reshape((N_SECTION, -1) + values.shape[1:])
    return jnp.roll(shaped, 3, axis=0).reshape(values.shape)

def attend_block(pieces, causal):
    query, keys, values, seg_query, seg_keys = pieces
    score = low_back(jnp.einsum('qhd,khd->hqk', query, keys, precision=lax.Precision.HIGHEST))
    allow = seg_query[:, None] == seg_keys[None, :]
    if causal:
        rows = lax.broadcasted_iota(jnp.int32, allow.shape, 0)
        cols = lax.broadcasted_iota(jnp.int32, allow.shape, 1)
        allow = allow & (rows >= cols)
    score = jnp.where(allow[None], score, -1e+30)
    top = lax.optimization_barrier(jnp.max(score, axis=-1, keepdims=True))
    expo = jnp.exp(score - top)
    prob = expo / lax.optimization_barrier(jnp.sum(expo, axis=-1, keepdims=True))
    return jnp.einsum('hqk,khd->qhd', low(prob), values, precision=lax.Precision.HIGHEST)

def attention(x_low, kv_low, w_in, w_out, bias, out_shift, seg_query, seg_keys, causal):
    query = low(low_back((matmul(x_low, w_in[0]) + bias[0]) * 0.125))
    keys = low(low_back(matmul(kv_low, w_in[1])))
    values = low(low_back(matmul(kv_low, w_in[2]) + bias[1]))
    blocks = query.shape[0] // TOK_DEV
    shaped = (query.reshape(blocks, TOK_DEV, HEADS, HEAD_DIM), keys.reshape(blocks, TOK_DEV, HEADS, HEAD_DIM), values.reshape(blocks, TOK_DEV, HEADS, HEAD_DIM), seg_query.reshape(blocks, TOK_DEV), seg_keys.reshape(blocks, TOK_DEV))
    context = lax.map(jax.checkpoint(partial(attend_block, causal=causal)), shaped)
    context = low(low_back(context.reshape(-1, D)))
    return low_back(matmul(context, w_out)) + out_shift

def feed(x_low, w_up, b_up, w_down, out_shift):
    pre = low_back(matmul(x_low, w_up) + b_up)
    act = low(jax.nn.gelu(pre, approximate=False))
    return low_back(matmul(act, w_down)) + out_shift

def rounded(value):
    return low_back(low(value))

def forward(source, target, attn_in, attn_out, w_up, w_down, qv_bias, up_bias, gains, shifts, src_seg, tgt_seg):
    qv_rows = qv_bias.reshape(3, 2, D)
    up_rows = up_bias.reshape(2, FF)
    source_low = low(source)
    resid0 = source + attention(source_low, source_low, attn_in[0], attn_out[0], qv_rows[0], shifts[5], src_seg, src_seg, False)
    hidden0 = rounded(layer_norm(resid0, gains[0], shifts[0]))
    resid1 = hidden0 + feed(hidden0, w_up[0], up_rows[0], w_down[0], shifts[8])
    encoded = rounded(layer_norm(resid1, gains[1], shifts[1]))
    target_low = low(target)
    resid2 = target + attention(target_low, target_low, attn_in[1], attn_out[1], qv_rows[1], shifts[6], tgt_seg, tgt_seg, True)
    hidden2 = rounded(layer_norm(resid2, gains[2], shifts[2]))
    resid3 = hidden2 + attention(hidden2, paired(encoded), attn_in[2], attn_out[2], qv_rows[2], shifts[7], tgt_seg, paired(src_seg), False)
    hidden3 = rounded(layer_norm(resid3, gains[3], shifts[3]))
    resid4 = hidden3 + feed(hidden3, w_up[1], up_rows[1], w_down[1], shifts[9])
    return low(layer_norm(resid4, gains[4], shifts[4]))

def reference(src_in, tgt_in, src_seg, tgt_seg, attn_in, attn_out, w_up, w_down, qv_bias, up_bias, gains, shifts, d_out):
    floats = tuple((item.astype(jnp.float32) for item in (src_in, tgt_in, attn_in, attn_out, w_up, w_down, qv_bias, up_bias, gains, shifts)))

    def wrapped(*params):
        return forward(*params, src_seg, tgt_seg)
    output, pull = jax.vjp(wrapped, *floats)
    grads = pull(d_out.astype(jnp.float32))
    return (output.astype(jnp.bfloat16), grads[0], grads[1], grads[2], grads[3], grads[4], grads[5], grads[6], grads[7], grads[8], grads[9])
```

```python
import jax
import jax.numpy as jnp
from jax import lax
from jax.sharding import PartitionSpec as P

HEAD_DIM = 64
LANE = 8


def shortened(shard):
    return jax.tree.map(lambda a: a.astype(jnp.bfloat16) if a.dtype == jnp.float32 else a, shard)


def passed_along(value, axis, steps):
    count = lax.axis_size(axis)
    pairs = [(source, (source + steps) % count) for source in range(count)]
    return lax.ppermute(value, axis, pairs)


def from_behind(value, axis, steps):
    count = lax.axis_size(axis)
    first, last = (max(0, -steps), min(count, count - steps))
    return lax.ppermute(value, axis, [(source, source + steps) for source in range(first, last)])


def layer_norm(resid, gain, shift):
    center = resid - jnp.mean(resid, axis=-1, keepdims=True)
    spread = jnp.mean(center * center, axis=-1, keepdims=True)
    return center * lax.rsqrt(spread + 1e-05) * gain + shift


def gelu_exact(value):
    return jax.nn.gelu(value, approximate=False)


def project(rows, weight):
    return jnp.dot(rows, weight, preferred_element_type=jnp.float32)


def sum_heads(partial_sum):
    return jax.tree.map(
        lambda part: part.astype(jnp.float32), lax.psum(shortened(partial_sum), "tensor")
    )


def sum_back(partial_sums):
    return (
        lax.psum(partial_sums[0].astype(jnp.bfloat16), "tensor").astype(jnp.float32),
        lax.psum(partial_sums[1].astype(jnp.bfloat16), "tensor").astype(jnp.float32),
    )


def return_rows(packed):
    return lax.all_to_all(
        packed.astype(jnp.bfloat16), "section", split_axis=0, concat_axis=0, tiled=True
    ).astype(packed.dtype)


def send_home(value, amount, sections):
    steps = amount % sections
    return passed_along(value.astype(jnp.bfloat16), "section", steps).astype(value.dtype)


def allowed(seg_query, seg_keys, causal):
    allow = seg_query[:, None] == seg_keys[None, :]
    if causal:
        rows = lax.broadcasted_iota(jnp.int32, allow.shape, 0)
        cols = lax.broadcasted_iota(jnp.int32, allow.shape, 1)
        allow = allow & (rows >= cols)
    return allow


def attend_core(x_low, kv_low, in_w, att_bias, allow):
    half = in_w.shape[2]
    heads = half // HEAD_DIM
    rows_query = x_low.shape[0]
    rows_keys = kv_low.shape[0]
    query = ((project(x_low, in_w[0]) + att_bias[0].astype(jnp.float32)) * 0.125).astype(
        jnp.bfloat16
    )
    keys = project(kv_low, in_w[1]).astype(jnp.bfloat16)
    values = (project(kv_low, in_w[2]) + att_bias[1].astype(jnp.float32)).astype(jnp.bfloat16)
    score = jnp.einsum(
        "qhd,khd->hqk",
        query.reshape(rows_query, heads, HEAD_DIM),
        keys.reshape(rows_keys, heads, HEAD_DIM),
        preferred_element_type=jnp.float32,
    )
    score = jnp.where(allow[None], score, -1e30)
    top = jnp.max(score, axis=-1, keepdims=True)
    expo = jnp.exp(score - top)
    prob = expo / jnp.sum(expo, axis=-1, keepdims=True)
    prob_low = prob.astype(jnp.bfloat16)
    context = jnp.einsum(
        "hqk,khd->qhd",
        prob_low,
        values.reshape(rows_keys, heads, HEAD_DIM),
        preferred_element_type=jnp.float32,
    )
    context = context.reshape(rows_query, half).astype(jnp.bfloat16)
    return (query, keys, values, prob, prob_low, context)


def attend_backward(grad_low, saved, x_low, kv_low, in_w, out_w):
    query, keys, values, prob, prob_low, context = saved
    rows_query = query.shape[0]
    rows_keys = keys.shape[0]
    half = query.shape[1]
    heads = half // HEAD_DIM
    query_heads = query.reshape(rows_query, heads, HEAD_DIM)
    key_heads = keys.reshape(rows_keys, heads, HEAD_DIM)
    value_heads = values.reshape(rows_keys, heads, HEAD_DIM)
    grad_out_w = jnp.einsum("rd,re->de", context, grad_low, preferred_element_type=jnp.float32)
    d_context = jnp.einsum("re,de->rd", grad_low, out_w, preferred_element_type=jnp.float32).astype(
        jnp.bfloat16
    )
    d_context = d_context.reshape(rows_query, heads, HEAD_DIM)
    d_prob = jnp.einsum("qhd,khd->hqk", d_context, value_heads, preferred_element_type=jnp.float32)
    delta = jnp.sum(prob * d_prob, axis=-1, keepdims=True)
    d_score = (prob * (d_prob - delta)).astype(jnp.bfloat16)
    d_query = jnp.einsum(
        "hqk,khd->qhd", d_score, key_heads, preferred_element_type=jnp.float32
    ).astype(jnp.bfloat16)
    d_query = (d_query * 0.125).reshape(rows_query, half)
    d_keys = (
        jnp.einsum("hqk,qhd->khd", d_score, query_heads, preferred_element_type=jnp.float32)
        .astype(jnp.bfloat16)
        .reshape(rows_keys, half)
    )
    d_values = (
        jnp.einsum("hqk,qhd->khd", prob_low, d_context, preferred_element_type=jnp.float32)
        .astype(jnp.bfloat16)
        .reshape(rows_keys, half)
    )
    grad_in_w = jnp.stack(
        [
            jnp.einsum("rd,re->de", x_low, d_query, preferred_element_type=jnp.float32),
            jnp.einsum("rd,re->de", kv_low, d_keys, preferred_element_type=jnp.float32),
            jnp.einsum("rd,re->de", kv_low, d_values, preferred_element_type=jnp.float32),
        ]
    )
    grad_bias = jnp.stack(
        [
            jnp.sum(d_query.astype(jnp.float32), axis=0),
            jnp.sum(d_values.astype(jnp.float32), axis=0),
        ]
    )
    d_x = jnp.einsum("re,de->rd", d_query, in_w[0], preferred_element_type=jnp.float32)
    d_kv = jnp.einsum("re,de->rd", d_keys, in_w[1], preferred_element_type=jnp.float32)
    d_kv = d_kv + jnp.einsum("re,de->rd", d_values, in_w[2], preferred_element_type=jnp.float32)
    return (d_x, d_kv, grad_in_w, grad_out_w, grad_bias)


def feed_core(x_low, up_mat, up_vec):
    pre = project(x_low, up_mat) + up_vec.astype(jnp.float32)
    return (pre, gelu_exact(pre).astype(jnp.bfloat16))


def feed_backward(grad_low, pre, act_low, x_low, up_mat, down_mat):
    grad_down = jnp.einsum("rf,rd->fd", act_low, grad_low, preferred_element_type=jnp.float32)
    d_act = jnp.einsum("rd,fd->rf", grad_low, down_mat, preferred_element_type=jnp.float32)
    value, pull = jax.vjp(gelu_exact, pre)
    d_pre = pull(d_act)[0].astype(jnp.bfloat16)
    grad_up = jnp.einsum("rd,rf->df", x_low, d_pre, preferred_element_type=jnp.float32)
    grad_up_vec = jnp.sum(d_pre.astype(jnp.float32), axis=0)
    d_x = jnp.einsum("rf,df->rd", d_pre, up_mat, preferred_element_type=jnp.float32)
    return (d_x, grad_up, grad_up_vec, grad_down)


def norm_backward(resid, gain, shift, grad):
    value, pull = jax.vjp(layer_norm, resid, gain, shift)
    return pull(grad)


def vector_share(qv_bias, up_bias, gains, shifts):
    return jnp.concatenate(
        [gains.reshape(-1), shifts.reshape(-1), qv_bias.reshape(-1), up_bias.reshape(-1)]
    )


def local(
    src_in,
    tgt_in,
    src_seg,
    tgt_seg,
    attn_in,
    attn_out,
    w_up,
    w_down,
    qv_bias,
    up_bias,
    gains,
    shifts,
    d_out,
):
    sections = lax.axis_size("section")
    place = lax.axis_index("section")
    replica = lax.axis_index("dp")
    replicas = lax.axis_size("dp")
    rows = src_in.shape[0]
    width = src_in.shape[1]
    piece = width // sections
    half = attn_in.shape[3]
    ff_half = w_up.shape[2]
    groups = up_bias.shape[1]
    heads = qv_bias.shape[2]
    bit = qv_bias.shape[3]
    tgt_low = passed_along(tgt_in, "section", -3)
    top_low = passed_along(d_out, "section", -3)
    src_low = src_in

    def gathered(share):
        return lax.all_gather(share, "section", axis=0, tiled=True)

    att_w = [
        gathered(jnp.concatenate([attn_in[a, 0], attn_in[a, 1], attn_in[a, 2], attn_out[a].T], 1))
        for a in range(3)
    ]
    ffn_w = [gathered(jnp.concatenate([w_up[f], w_down[f].T], 1)) for f in range(2)]
    vectors = gathered(vector_share(qv_bias, up_bias, gains, shifts)[None])
    norm_vec = vectors[:, : 15 * piece].reshape(sections, 15, piece).transpose(1, 0, 2)
    norm_vec = norm_vec.reshape(15, width).astype(jnp.float32)
    gain, shift = norm_vec[:5], norm_vec[5:]
    stop = 15 * piece + 6 * heads * bit
    qv_vec = vectors[:, 15 * piece : stop].reshape(sections, 3, 2, heads, bit)
    qv_vec = qv_vec.transpose(1, 2, 3, 0, 4).reshape(3, 2, half)
    up_vec = vectors[:, stop:].reshape(sections, 2, groups, bit).transpose(1, 2, 0, 3)
    up_vec = up_vec.reshape(2, ff_half)

    in_w = [att_w[a][:, : 3 * half].reshape(width, 3, half).transpose(1, 0, 2) for a in range(3)]
    out_w = [att_w[a][:, 3 * half :].T for a in range(3)]
    up_w = [ffn_w[f][:, :ff_half] for f in range(2)]
    down_w = [ffn_w[f][:, ff_half:].T for f in range(2)]
    own_src = src_seg.reshape(sections, replicas, rows)[place, replica]
    own_tgt = tgt_seg.reshape(sections, replicas, rows)[(place + 3) % sections, replica]
    allow = [
        allowed(own_src, own_src, False),
        allowed(own_tgt, own_tgt, True),
        allowed(own_tgt, own_src, False),
    ]

    def attend(a, x_low, y_low):
        saved = attend_core(x_low, y_low, in_w[a], qv_vec[a], allow[a])
        return saved, sum_heads(project(saved[5], out_w[a]))

    def feed(f, x_low):
        pre, act_low = feed_core(x_low, up_w[f], up_vec[f])
        return (pre, act_low), sum_heads(project(act_low, down_w[f]))

    def normed(resid, index):
        return layer_norm(resid, gain[index], shift[index]).astype(jnp.bfloat16)

    saved0, branch = attend(0, src_low, src_low)
    resid0 = src_low.astype(jnp.float32) + (branch + shift[5])
    hidden0 = normed(resid0, 0)
    saved2, branch = attend(1, tgt_low, tgt_low)
    resid2 = tgt_low.astype(jnp.float32) + (branch + shift[6])
    hidden2 = normed(resid2, 2)
    saved1, branch = feed(0, hidden0)
    resid1 = hidden0.astype(jnp.float32) + (branch + shift[8])
    encoded = normed(resid1, 1)
    saved3, branch = attend(2, hidden2, encoded)
    resid3 = hidden2.astype(jnp.float32) + (branch + shift[7])
    hidden3 = normed(resid3, 3)
    saved4, branch = feed(1, hidden3)
    resid4 = hidden3.astype(jnp.float32) + (branch + shift[9])
    dec_out = passed_along(normed(resid4, 4), "section", 3)

    def back(index, resid, grad):
        d_resid, d_gain, d_shift = norm_backward(resid, gain[index], shift[index], grad)
        return d_resid, d_gain, d_shift, jnp.sum(d_resid, axis=0)

    def one_sum(part):
        return lax.psum(part.astype(jnp.bfloat16), "tensor").astype(jnp.float32)

    def rounded(value):
        return value.astype(jnp.bfloat16).astype(jnp.float32)

    def scattered(grad):
        share = lax.psum_scatter(
            grad.astype(jnp.bfloat16), "section", scatter_dimension=0, tiled=True
        )
        return lax.psum(share, "dp").astype(jnp.float32)

    def feed_grads(f, d_resid, saved, x_low):
        d_x, g_up, g_vec, g_down = feed_backward(
            d_resid.astype(jnp.bfloat16), saved[0], saved[1], x_low, up_w[f], down_w[f]
        )
        return one_sum(d_x), scattered(jnp.concatenate([g_up, g_down.T], 1)), g_vec

    def attend_grads(a, d_resid, saved, x_low, y_low):
        d_x, d_y, g_in, g_out, g_bias = attend_backward(
            d_resid.astype(jnp.bfloat16), saved, x_low, y_low, in_w[a], out_w[a]
        )
        joined = jnp.concatenate([g_in[0], g_in[1], g_in[2], g_out.T], 1)
        return d_x, d_y, scattered(joined), g_bias

    side = [None] * 5
    d_resid, *side[4] = back(4, resid4, top_low.astype(jnp.float32))
    d_x, ffn_g1, vec_g1 = feed_grads(1, d_resid, saved4, hidden3)
    d_resid, *side[3] = back(3, resid3, rounded(d_resid + d_x))
    d_x, d_y, att_g2, bias_g2 = attend_grads(2, d_resid, saved3, hidden2, encoded)
    d_x, d_y = one_sum(d_x), one_sum(d_y)
    d_enc, *side[1] = back(1, resid1, rounded(d_y))
    d_resid, *side[2] = back(2, resid2, rounded(d_resid + d_x))
    d_x, ffn_g0, vec_g0 = feed_grads(0, d_enc, saved1, hidden0)
    d_enc, *side[0] = back(0, resid0, rounded(d_enc + d_x))
    d_x, d_y, att_g1, bias_g1 = attend_grads(1, d_resid, saved2, tgt_low, tgt_low)
    grad_tgt = passed_along((d_resid + one_sum(d_x + d_y)).astype(jnp.bfloat16), "section", 3)
    d_x, d_y, att_g0, bias_g0 = attend_grads(0, d_enc, saved0, src_low, src_low)
    grad_src = d_enc + one_sum(d_x + d_y)

    order = [0, 2, 3, 1, 4]
    side_g = jnp.stack([s[0] for s in side] + [s[1] for s in side] + [side[i][2] for i in order])
    side_g = side_g.reshape(15, sections, piece).transpose(1, 0, 2).reshape(sections, -1)
    qv_g = jnp.stack([bias_g0, bias_g1, bias_g2]).reshape(3, 2, heads, sections, bit)
    qv_g = qv_g.transpose(3, 0, 1, 2, 4).reshape(sections, -1)
    up_g = jnp.stack([vec_g0, vec_g1]).reshape(2, groups, sections, bit)
    up_g = up_g.transpose(2, 0, 1, 3).reshape(sections, -1)
    vec = scattered(jnp.concatenate([side_g, qv_g, up_g], 1))[0]
    att_g = [att_g0, att_g1, att_g2]
    ffn_g = [ffn_g0, ffn_g1]
    grad_attn_in = jnp.stack(
        [g[:, : 3 * half].reshape(piece, 3, half).transpose(1, 0, 2) for g in att_g]
    )
    return (
        dec_out,
        grad_src,
        grad_tgt.astype(jnp.float32),
        grad_attn_in,
        jnp.stack([g[:, 3 * half :].T for g in att_g]),
        jnp.stack([g[:, :ff_half] for g in ffn_g]),
        jnp.stack([g[:, ff_half:].T for g in ffn_g]),
        vec[15 * piece : stop].reshape(3, 2, heads, bit),
        vec[stop:].reshape(2, groups, bit),
        vec[: 5 * piece].reshape(5, piece),
        vec[5 * piece : 15 * piece].reshape(10, piece),
    )


def solution(mesh):
    placed = (
        P(("section", "dp"), None),
        P(("section", "dp"), None),
        P(),
        P(),
        P(None, None, "section", "tensor"),
        P(None, "tensor", "section"),
        P(None, "section", "tensor"),
        P(None, "tensor", "section"),
        P(None, None, "tensor", "section"),
        P(None, "tensor", "section"),
        P(None, "section"),
        P(None, "section"),
        P(("section", "dp"), None),
    )
    return jax.shard_map(
        local,
        mesh=mesh,
        in_specs=placed,
        out_specs=(
            P(("section", "dp"), None),
            P(("section", "dp"), None),
            P(("section", "dp"), None),
            P(None, None, "section", "tensor"),
            P(None, "tensor", "section"),
            P(None, "section", "tensor"),
            P(None, "tensor", "section"),
            P(None, None, "tensor", "section"),
            P(None, "tensor", "section"),
            P(None, "section"),
            P(None, "section"),
        ),
        check_vma=False,
    )
```

```python
import jax
import jax.numpy as jnp
import numpy as np
from jax import lax
from jax.experimental import pallas as pl
from jax.experimental.pallas import tpu as pltpu
from jax.sharding import PartitionSpec as P

LOW = jnp.bfloat16
F32 = jnp.float32
MESH = pl.DeviceIdType.MESH
D = 768
HEAD = 64
BLOCK = 128
ROWS = 2 * BLOCK
PIECE = 24
CHIP = 48
HEADS = 3
STEP = 32

WIDE = (896, 768, 1536, 768, 1536)
FROM = (0, 896, 1664, 3200, 3968)
ALL = 5504
CUT = {896: (256, 384, 640), 768: (256, 384, 640), 1536: (384, 768, 1152)}
ATT_CHUNK = (0, 1, 3)
FFN_CHUNK = (2, 4)
VEC_QV = 16
VEC_UP = 34
OUT_ROW = (10, 13, 11, 12, 14)
N_SUM = 11
N_SEM = 216


def nn(left, right):
    return jnp.dot(left, right, preferred_element_type=F32)


def nt(left, right):
    return lax.dot_general(left, right, (((1,), (1,)), ((), ())), preferred_element_type=F32)


def tn(left, right):
    return lax.dot_general(left, right, (((0,), (0,)), ((), ())), preferred_element_type=F32)


def normal_part(value):
    return 0.5 * (1.0 + lax.erf(value * 0.7071067811865476))


def layers(*refs):
    refs = list(refs)

    def take(count):
        part, refs[:] = refs[:count], refs[count:]
        return part

    pack, src_in, tgt_in, d_out, src_seg, tgt_seg, pick = take(7)
    dec_out, grad_src, grad_tgt = take(3)
    out = take(5)
    w, g, r1, r2, q1, q2, dsnd, drcv, tot = [take(5) for _ in range(9)]
    snd1, rcv1, snd2, rcv2, own = [take(N_SUM) for _ in range(5)]
    both, src2, tgt2, h0, enc, h2, h3, dgot, dec_snd, tgt_snd = take(10)
    gl, gres, hat, rstd = [take(5) for _ in range(4)]
    qkv, prob, ctx, dqkv, bias = [take(3) for _ in range(5)]
    pre, act, dpre, up_row, up_sum = [take(2) for _ in range(5)]
    vec, side, bias_sum, flat = take(4)
    send_sem, recv_sem, local_sem = take(3)

    me = lax.axis_index("section")
    z, y, c = me // 8, lax.rem(me // 2, 4), lax.rem(me, 2)
    chip = me // 2
    replica = lax.axis_index("dp")
    zp, zm, z2 = lax.rem(z + 1, 4), lax.rem(z + 3, 4), lax.rem(z + 2, 4)
    yp, ym, y2 = lax.rem(y + 1, 4), lax.rem(y + 3, 4), lax.rem(y + 2, 4)

    def at(zz, yy):
        return {"section": zz * 8 + yy * 2 + c}

    dzp, dzm, dyp, dym = at(zp, y), at(zm, y), at(z, yp), at(z, ym)
    twin = {"section": me + 1 - 2 * c}
    beside = {"tensor": 1 - lax.axis_index("tensor")}
    partner = {"dp": 1 - replica}
    behind = {"section": lax.rem(me + 29, 32)}
    ahead = {"section": lax.rem(me + 3, 32)}
    mine = pl.multiple_of(c * BLOCK, BLOCK)
    theirs = pl.multiple_of((1 - c) * BLOCK, BLOCK)
    my_rows, their_rows = pl.ds(mine, BLOCK), pl.ds(theirs, BLOCK)

    barrier = pltpu.get_barrier_semaphore()
    for device in (dzp, dzm, dyp, dym, twin, beside, partner, behind, ahead):
        pl.semaphore_signal(barrier, inc=1, device_id=device, device_id_type=MESH)
    pl.semaphore_wait(barrier, 9)

    started = []

    def send(src, dst, device):
        index = len(started)
        copy = pltpu.make_async_remote_copy(
            src_ref=src,
            dst_ref=dst,
            send_sem=send_sem.at[index],
            recv_sem=recv_sem.at[index],
            device_id=device,
            device_id_type=MESH,
        )
        started.append(copy)
        copy.start()
        return copy

    def halves(k):
        a1, a2, b1 = CUT[WIDE[k]]
        n = WIDE[k]
        return (
            pl.ds(0, a2),
            pl.ds(a2, n - a2),
            pl.ds(0, a1),
            pl.ds(a1, a2 - a1),
            pl.ds(a2, b1 - a2),
            pl.ds(b1, n - b1),
        )

    lo, hi = pl.ds(0, 2), pl.ds(2, 2)
    first, second, third, fourth = {}, {}, {}, {}

    def gather0(k):
        a, b = halves(k)[:2]
        cols = slice(FROM[k], FROM[k] + WIDE[k])
        shard_copy[k].wait_recv()
        joined = jnp.concatenate(
            [both[0, :PIECE, cols].astype(F32), both[1, :PIECE, cols].astype(F32)], axis=0
        )
        w[k][z, y] = joined.astype(LOW)
        src_a, src_b = w[k].at[z, y, :, a], w[k].at[z, y, :, b]
        first[k] = [
            send(src_a, src_a, dzp),
            send(src_b, src_b, dyp),
            send(src_a, src_a, dzm),
            send(src_b, src_b, dym),
        ]

    def gather1(k):
        ap, am, bp, bm = halves(k)[2:]
        second[k] = []
        order = (
            (w[k].at[zm, y, :, ap], dzp),
            (w[k].at[z, ym, :, bp], dyp),
            (w[k].at[zp, y, :, am], dzm),
            (w[k].at[z, yp, :, bm], dym),
        )
        for copy, (block, device) in zip(first[k], order):
            copy.wait_recv()
            second[k].append(send(block, block, device))

    def gather2(k):
        a, b = halves(k)[:2]
        for copy in second[k]:
            copy.wait_recv()
        row, line = w[k].at[:, y, :, a], w[k].at[z, :, :, b]
        third[k] = [
            send(row, row, dyp),
            send(line, line, dzp),
            send(row, row, dym),
            send(line, line, dzm),
        ]

    def gather3(k):
        a, b = halves(k)[:2]
        fourth[k] = []
        order = (
            (w[k].at[lo, ym, :, a], dyp),
            (w[k].at[zm, lo, :, b], dzp),
            (w[k].at[hi, yp, :, a], dym),
            (w[k].at[zp, hi, :, b], dzm),
        )
        for copy, (block, device) in zip(third[k], order):
            copy.wait_recv()
            fourth[k].append(send(block, block, device))

    def gather4(k):
        for copy in fourth[k]:
            copy.wait_recv()

    def weight(k, start, stop):
        return w[k][:, :, :, start:stop].reshape(D, stop - start)

    down1, down2, down3, down4, down5, down6 = {}, {}, {}, {}, {}, {}

    def scatter0(k):
        a, b = halves(k)[:2]
        na, nb = pl.ds(0, a.size), pl.ds(0, b.size)
        down1[k] = [
            send(g[k].at[z2, lo, :, a], r1[k].at[0, :, :, na], dzp),
            send(g[k].at[lo, y2, :, b], r1[k].at[1, :, :, nb], dyp),
            send(g[k].at[z2, hi, :, a], r1[k].at[2, :, :, na], dzm),
            send(g[k].at[hi, y2, :, b], r1[k].at[3, :, :, nb], dym),
        ]

    def scatter1(k):
        a, b = halves(k)[:2]
        na, nb = pl.ds(0, a.size), pl.ds(0, b.size)
        copies, down2[k] = down1[k], []
        copies[0].wait_recv()
        g[k][zp, lo, :, a] += r1[k][0, :, :, na]
        down2[k].append(send(g[k].at[zp, :, :, a], r2[k].at[0, :, :, na], dzp))
        copies[1].wait_recv()
        g[k][lo, yp, :, b] += r1[k][1, :, :, nb]
        down2[k].append(send(g[k].at[:, yp, :, b], r2[k].at[1, :, :, nb], dyp))
        copies[2].wait_recv()
        g[k][zm, hi, :, a] += r1[k][2, :, :, na]
        down2[k].append(send(g[k].at[zm, :, :, a], r2[k].at[2, :, :, na], dzm))
        copies[3].wait_recv()
        g[k][hi, ym, :, b] += r1[k][3, :, :, nb]
        down2[k].append(send(g[k].at[:, ym, :, b], r2[k].at[3, :, :, nb], dym))

    def scatter2(k):
        a, b, ap, am, bp, bm = halves(k)
        na, nb = pl.ds(0, a.size), pl.ds(0, b.size)
        copies = down2[k]
        copies[0].wait_recv()
        copies[2].wait_recv()
        g[k][z, :, :, a] += r2[k][0, :, :, na] + r2[k][2, :, :, na]
        down3[k] = [
            send(g[k].at[z, y2, :, ap], q1[k].at[0, :, pl.ds(0, ap.size)], dyp),
            send(g[k].at[z, y2, :, am], q1[k].at[1, :, pl.ds(0, am.size)], dym),
        ]
        copies[1].wait_recv()
        copies[3].wait_recv()
        g[k][:, y, :, b] += r2[k][1, :, :, nb] + r2[k][3, :, :, nb]
        down3[k] += [
            send(g[k].at[z2, y, :, bp], q1[k].at[2, :, pl.ds(0, bp.size)], dzp),
            send(g[k].at[z2, y, :, bm], q1[k].at[3, :, pl.ds(0, bm.size)], dzm),
        ]

    def scatter3(k):
        a, b, ap, am, bp, bm = halves(k)
        na, nb = pl.ds(0, a.size), pl.ds(0, b.size)
        copies, down4[k] = down3[k], []
        copies[0].wait_recv()
        g[k][z, yp, :, ap] += q1[k][0, :, : ap.size]
        down4[k].append(send(g[k].at[z, yp, :, a], q2[k].at[0, :, na], dyp))
        copies[1].wait_recv()
        g[k][z, ym, :, am] += q1[k][1, :, : am.size]
        down4[k].append(send(g[k].at[z, ym, :, a], q2[k].at[1, :, na], dym))
        copies[2].wait_recv()
        g[k][zp, y, :, bp] += q1[k][2, :, : bp.size]
        down4[k].append(send(g[k].at[zp, y, :, b], q2[k].at[2, :, nb], dzp))
        copies[3].wait_recv()
        g[k][zm, y, :, bm] += q1[k][3, :, : bm.size]
        down4[k].append(send(g[k].at[zm, y, :, b], q2[k].at[3, :, nb], dzm))

    def scatter4(k):
        a, b = halves(k)[:2]
        for copy in down4[k]:
            copy.wait_recv()
        for cols, i in ((a, 0), (b, 2)):
            n = pl.ds(0, cols.size)
            got = q2[k][i, :, n].astype(F32) + q2[k][i + 1, :, n].astype(F32)
            dsnd[k][:, cols] = (g[k][z, y, :, cols].astype(F32) + got).astype(LOW)
        down5[k] = send(dsnd[k], drcv[k], partner)

    def scatter5(k):
        down5[k].wait_recv()
        tot[k][...] = dsnd[k][...].astype(F32) + drcv[k][...].astype(F32)
        rows_mine = pl.ds(pl.multiple_of(c * PIECE, PIECE), PIECE)
        rows_theirs = pl.ds(pl.multiple_of((1 - c) * PIECE, PIECE), PIECE)
        down6[k] = send(tot[k].at[rows_theirs], out[k].at[c], twin)
        out[k][c] = tot[k][rows_mine, :]

    def scatter6(k):
        down6[k].wait_recv()

    def put_grad(k, start, value):
        n = value.shape[1]
        g[k][:, :, :, start : start + n] = value.astype(LOW).reshape(4, 4, CHIP, n)

    hop1, hop2 = {}, {}

    def sum0(i, part):
        snd1[i][...] = part(their_rows).astype(LOW)
        hop1[i] = send(snd1[i], rcv1[i], twin)
        own[i][...] = part(my_rows)

    def sum1(i):
        hop1[i].wait_recv()
        snd2[i][...] = (own[i][...] + rcv1[i][...].astype(F32)).astype(LOW)
        hop2[i] = send(snd2[i], rcv2[i], beside)

    def sum2(i):
        hop2[i].wait_recv()

    def summed(i, rows):
        return snd2[i][rows, :].astype(F32) + rcv2[i][rows, :].astype(F32)

    shared = {}

    def share(name, ref):
        view = ref.at[my_rows]
        shared[name] = send(view, view, twin)

    def share_wait(name):
        shared[name].wait_recv()

    def norm(i, n, x_ref, out_ref):
        gain, shift, out_shift = (vec[r : r + 1, :] for r in (n, 5 + n, OUT_ROW[n]))
        for r in range(0, BLOCK, STEP):
            rows = pl.ds(r, STEP)
            place = pl.ds(pl.multiple_of(mine + r, STEP), STEP)
            resid = x_ref[place, :].astype(F32) + (summed(i, rows) + out_shift)
            center = resid - jnp.mean(resid, axis=1, keepdims=True)
            spread = jnp.mean(center * center, axis=1, keepdims=True)
            scale = lax.rsqrt(spread + 1e-05)
            hat[n][rows, :] = center * scale
            rstd[n][rows, :] = scale
            result = (center * scale * gain + shift).astype(LOW)
            if out_ref is None:
                dec_snd[rows, :] = result
            else:
                out_ref[place, :] = result

    def norm_back(n, top):
        gain = vec[n : n + 1, :]
        sums = [jnp.zeros((8, D), F32) for _ in range(3)]
        for r in range(0, BLOCK, STEP):
            rows = pl.ds(r, STEP)
            place = pl.ds(pl.multiple_of(mine + r, STEP), STEP)
            grad = top(rows)
            x_hat = hat[n][rows, :]
            d_hat = grad * gain
            mean1 = jnp.mean(d_hat, axis=1, keepdims=True)
            mean2 = jnp.mean(d_hat * x_hat, axis=1, keepdims=True)
            resid = rstd[n][rows, :] * (d_hat - mean1 - x_hat * mean2)
            gres[n][rows, :] = resid
            gl[n][place, :] = resid.astype(LOW)
            for j, value in enumerate((grad * x_hat, grad, resid)):
                sums[j] = sums[j] + jnp.sum(value.reshape(STEP // 8, 8, D), axis=0)
        share(("gl", n), gl[n])
        for row, value in zip((n, 5 + n, OUT_ROW[n]), sums):
            side[row : row + 1, :] = jnp.sum(value, axis=0, keepdims=True)

    def lanes(start, width):
        return lax.broadcasted_iota(jnp.int32, (1, width), 1) + start

    def segment_row(table, shift, half):
        section = lax.rem(2 * chip + half + shift, 32)
        row = table[pl.ds(2 * section + replica, 1), :].astype(F32)
        return jnp.broadcast_to(row, (BLOCK, BLOCK))

    def allowed(a, half):
        query = segment_row(src_seg, 0, half) if a == 0 else segment_row(tgt_seg, 3, half)
        keys = segment_row(tgt_seg, 3, half) if a == 1 else segment_row(src_seg, 0, half)
        allow = query.T == keys
        if a == 1:
            row = lax.broadcasted_iota(jnp.int32, (BLOCK, BLOCK), 0)
            col = lax.broadcasted_iota(jnp.int32, (BLOCK, BLOCK), 1)
            allow = allow & (row >= col)
        return allow

    def heads_of(a, rows, head):
        return (qkv[a][rows, s + head * HEAD : s + (head + 1) * HEAD] for s in (0, 192, 384))

    def attend(a, x_ref, y_ref):
        k = ATT_CHUNK[a]
        scale = jnp.where(lanes(0, 640) < 192, 0.125, 1.0)
        row_bias = bias[a][0:1, :]
        if a < 2:
            joined = nn(x_ref[...], weight(k, 0, 640))
        else:
            left = nn(x_ref[...], weight(k, 0, 256))
            right = nn(y_ref[...], weight(k, 128, 640))
            middle = jnp.where(lanes(128, 128) < 192, left[:, 128:], right[:, :128])
            joined = jnp.concatenate([left[:, :128], middle, right[:, 128:]], axis=1)
        qkv[a][...] = ((joined + row_bias) * scale).astype(LOW)
        for half in range(2):
            rows = slice(half * BLOCK, (half + 1) * BLOCK)
            allow = allowed(a, half)
            parts = [jnp.zeros((BLOCK, HEAD), LOW)]
            for head in range(HEADS):
                q, key, v = heads_of(a, rows, head)
                score = jnp.where(allow, nt(q, key), -1e30)
                expo = jnp.exp(score - jnp.max(score, axis=1, keepdims=True))
                p = expo / jnp.sum(expo, axis=1, keepdims=True)
                prob[a][half * HEADS + head] = p
                parts.append(nn(p.astype(LOW), v).astype(LOW))
            ctx[a][rows, :] = jnp.concatenate(parts, axis=1)

    def attend_out(a):
        k = ATT_CHUNK[a]
        return lambda rows: nt(ctx[a][rows, :], weight(k, 512, 768))

    def attend_back(a, n):
        k = ATT_CHUNK[a]
        d_ctx = nn(gl[n][...], weight(k, 512, 768)).astype(LOW)
        for half in range(2):
            rows = slice(half * BLOCK, (half + 1) * BLOCK)
            d_q, d_k, d_v = [], [], []
            for head in range(HEADS):
                q, key, v = heads_of(a, rows, head)
                d_c = d_ctx[rows, HEAD * (head + 1) : HEAD * (head + 2)]
                p = prob[a][half * HEADS + head]
                d_p = nt(d_c, v)
                delta = jnp.sum(p * d_p, axis=1, keepdims=True)
                d_s = (p * (d_p - delta)).astype(LOW)
                d_q.append((nn(d_s, key).astype(LOW).astype(F32) * 0.125).astype(LOW))
                d_k.append(tn(d_s, q).astype(LOW))
                d_v.append(tn(p.astype(LOW), d_c).astype(LOW))
            blank = jnp.zeros((BLOCK, HEAD), LOW)
            dqkv[a][rows, :] = jnp.concatenate(d_q + d_k + d_v + [blank], axis=1)
        total = jnp.sum(dqkv[a][...].astype(F32).reshape(ROWS // 8, 8, 640), axis=0)
        bias_sum[a : a + 1, :] = jnp.sum(total, axis=0, keepdims=True)

    def query_part(value):
        return jnp.where(lanes(0, 256) < 192, value.astype(F32), 0.0).astype(LOW)

    def key_part(value, start):
        return jnp.where(lanes(start, value.shape[1]) < 192, 0.0, value.astype(F32)).astype(LOW)

    def self_grad(a):
        k = ATT_CHUNK[a]
        return lambda rows: nt(dqkv[a][rows, :], weight(k, 0, 640))

    def cross_grad_x(rows):
        return nt(query_part(dqkv[2][rows, 0:256]), weight(3, 0, 256))

    def cross_grad_y(rows):
        return nt(key_part(dqkv[2][rows, 128:640], 128), weight(3, 128, 640))

    def attend_weights(a, x_ref, y_ref):
        k = ATT_CHUNK[a]
        if a < 2:
            put_grad(k, 0, tn(x_ref[...], dqkv[a][:, 0:512]))
        else:
            left = tn(x_ref[...], query_part(dqkv[a][:, 0:256]))
            put_grad(k, 0, left + tn(y_ref[...], key_part(dqkv[a][:, 0:256], 0)))
            put_grad(k, 256, tn(y_ref[...], dqkv[a][:, 256:512]))

    def attend_weights_out(a, n, y_ref):
        k = ATT_CHUNK[a]
        tail = jnp.concatenate([dqkv[a][:, 512:640], jnp.zeros((ROWS, 128), LOW)], axis=1)
        put_grad(k, 512, tn(y_ref[...], tail) + tn(gl[n][...], ctx[a][...]))

    def feed(f, x_ref):
        k = FFN_CHUNK[f]
        pre[f][...] = nn(x_ref[...], weight(k, 0, D)) + up_row[f][0:1, :]

        @pl.loop(0, ROWS // 16)
        def _(step):
            rows = pl.ds(pl.multiple_of(step * 16, 16), 16)
            value = pre[f][rows, :]
            act[f][rows, :] = (value * normal_part(value)).astype(LOW)

    def feed_slope(f):
        @pl.loop(0, ROWS // 16)
        def _(step):
            rows = pl.ds(pl.multiple_of(step * 16, 16), 16)
            value = pre[f][rows, :]
            bell = jnp.exp(-0.5 * value * value) * 0.3989422804014327
            pre[f][rows, :] = normal_part(value) + value * bell

    def feed_out(f):
        k = FFN_CHUNK[f]
        return lambda rows: nt(act[f][rows, :], weight(k, D, 2 * D))

    def feed_back(f, n):
        k = FFN_CHUNK[f]
        d_act = nn(gl[n][...], weight(k, D, 2 * D))
        dpre[f][...] = (pre[f][...] * d_act).astype(LOW)

    def feed_grad(f):
        k = FFN_CHUNK[f]
        return lambda rows: nt(dpre[f][rows, :], weight(k, 0, D))

    def feed_up_weights(f, x_ref):
        put_grad(FFN_CHUNK[f], 0, tn(x_ref[...], dpre[f][...]))

    def feed_down_weights(f, n):
        put_grad(FFN_CHUNK[f], D, tn(gl[n][...], act[f][...]))
        total = jnp.sum(dpre[f][...].astype(F32).reshape(ROWS // 8, 8, D), axis=0)
        up_sum[f][0:1, :] = jnp.sum(total, axis=0, keepdims=True)

    def unpack_vectors():
        packed = weight(0, D, 896)
        vec[...] = packed.astype(F32).T[:16, :]
        flat[...] = tn(packed, pick[...])
        for a in range(3):
            r = VEC_QV + 6 * a
            zero = jnp.zeros((1, HEAD), F32)
            pieces = [flat[r + i : r + i + 1, :HEAD] for i in range(6)]
            row = jnp.concatenate(pieces[:3] + [zero] * 3 + pieces[3:] + [zero], axis=1)
            bias[a][0:1, :] = row
        for f in range(2):
            r = VEC_UP + 12 * f
            pieces = [flat[r + i : r + i + 1, :HEAD] for i in range(12)]
            up_row[f][0:1, :] = jnp.concatenate(pieces, axis=1)

    def pack_vector_grads():
        rows = []
        for a in range(3):
            for s in (0, 384):
                rows += [bias_sum[a : a + 1, s + i * HEAD : s + (i + 1) * HEAD] for i in range(3)]
        for f in range(2):
            rows += [up_sum[f][0:1, i * HEAD : (i + 1) * HEAD] for i in range(12)]
        rows.append(jnp.zeros((6, HEAD), F32))
        small = jnp.concatenate(rows, axis=0).astype(LOW)
        spread = nt(small, pick[:, :HEAD])
        table = jnp.concatenate([side[...], spread, jnp.zeros((64, D), F32)], axis=0)
        put_grad(0, D, table.T)

    local = pltpu.make_async_copy(pack.at[c], both.at[c], local_sem.at[0])
    local.start()
    shard_copy = {}

    def send_shard(k):
        cols = pl.ds(FROM[k], WIDE[k])
        shard_copy[k] = send(pack.at[1 - c, :, cols], both.at[c, :, cols], twin)

    send_shard(0)
    send_shard(1)
    src_copy = send(src_in, src2.at[my_rows], twin)
    tgt_copy = send(tgt_in, tgt2.at[their_rows], behind)
    for k in range(2, 5):
        send_shard(k)
    local.wait()
    gather0(0)
    gather0(1)
    src2[my_rows, :] = src_in[...]
    side[...] = jnp.zeros((16, D), F32)

    gather1(0)
    gather0(2)
    gather2(0)
    gather1(1)
    gather0(3)
    tgt_copy.wait_recv()
    share("tgt", tgt2)
    gather3(0)
    gather2(1)
    gather1(2)
    gather0(4)
    src_copy.wait_recv()

    gather4(0)
    unpack_vectors()
    attend(0, src2, src2)
    sum0(0, attend_out(0))
    gather3(1)
    gather2(2)
    gather1(3)
    sum1(0)
    share_wait("tgt")
    gather4(1)
    attend(1, tgt2, tgt2)
    sum0(1, attend_out(1))
    gather3(2)
    sum2(0)
    norm(0, 0, src2, h0)
    share("h0", h0)
    gather2(3)
    gather1(4)
    sum1(1)
    gather4(2)
    share_wait("h0")
    feed(0, h0)
    sum0(2, feed_out(0))
    gather3(3)
    sum2(1)
    norm(1, 2, tgt2, h2)
    share("h2", h2)
    sum1(2)
    gather2(4)
    feed_slope(0)
    gather4(3)
    share_wait("h2")
    sum2(2)
    norm(2, 1, h0, enc)
    share("enc", enc)
    gather3(4)
    d_out_copy = send(d_out, dgot, behind)
    share_wait("enc")
    attend(2, h2, enc)
    sum0(3, attend_out(2))
    sum1(3)
    sum2(3)
    norm(3, 3, h2, h3)
    share("h3", h3)
    gather4(4)
    share_wait("h3")
    feed(1, h3)
    sum0(4, feed_out(1))
    sum1(4)
    feed_slope(1)
    d_out_copy.wait_recv()
    sum2(4)
    norm(4, 4, h3, None)
    norm_back(4, lambda rows: dgot[rows, :].astype(F32))
    dec_copy = send(dec_snd, dec_out, ahead)

    def rounded(n, i):
        return lambda rows: (gres[n][rows, :] + summed(i, rows)).astype(LOW).astype(F32)

    share_wait(("gl", 4))
    feed_back(1, 4)
    sum0(5, feed_grad(1))
    feed_up_weights(1, h3)
    sum1(5)
    feed_down_weights(1, 4)
    scatter0(4)
    sum2(5)
    norm_back(3, rounded(4, 5))
    scatter1(4)
    share_wait(("gl", 3))
    attend_back(2, 3)
    sum0(6, cross_grad_y)
    sum0(7, cross_grad_x)
    attend_weights(2, h2, enc)
    sum1(6)
    sum1(7)
    attend_weights_out(2, 3, enc)
    scatter0(3)
    scatter2(4)
    sum2(6)
    norm_back(1, lambda rows: summed(6, rows).astype(LOW).astype(F32))
    scatter1(3)
    share_wait(("gl", 1))
    feed_back(0, 1)
    sum0(8, feed_grad(0))
    sum2(7)
    norm_back(2, rounded(3, 7))
    feed_up_weights(0, h0)
    sum1(8)
    feed_down_weights(0, 1)
    scatter0(2)
    scatter3(4)
    scatter2(3)
    share_wait(("gl", 2))
    attend_back(1, 2)
    sum0(9, self_grad(1))
    sum2(8)
    norm_back(0, rounded(1, 8))
    attend_weights(1, tgt2, tgt2)
    sum1(9)
    attend_weights_out(1, 2, tgt2)
    scatter0(1)
    scatter1(2)
    share_wait(("gl", 0))
    attend_back(0, 0)
    sum0(10, self_grad(0))
    attend_weights(0, src2, src2)
    sum1(10)
    attend_weights_out(0, 0, src2)
    pack_vector_grads()
    scatter0(0)
    scatter4(4)
    scatter3(3)
    scatter2(2)
    scatter1(1)
    sum2(9)
    for r in range(0, BLOCK, STEP):
        rows = pl.ds(r, STEP)
        tgt_snd[rows, :] = (gres[2][rows, :] + summed(9, rows)).astype(LOW)
    tgt_copy_back = send(tgt_snd, grad_tgt, ahead)
    sum2(10)
    for r in range(0, BLOCK, STEP):
        rows = pl.ds(r, STEP)
        grad_src[rows, :] = gres[0][rows, :] + summed(10, rows)
    scatter1(0)
    scatter4(3)
    scatter3(2)
    scatter2(1)
    scatter2(0)
    scatter5(4)
    scatter5(3)
    scatter4(2)
    scatter3(1)
    scatter3(0)
    scatter5(2)
    scatter4(1)
    scatter4(0)
    scatter5(1)
    scatter5(0)
    for k in range(5):
        scatter6(k)
    dec_copy.wait_recv()
    tgt_copy_back.wait_recv()
    for copy in started:
        copy.wait_send()


def run_layers(pack, src_in, tgt_in, d_out, src_seg, tgt_seg, pick):
    def low(*shape):
        return pltpu.VMEM(shape, LOW)

    def wide(*shape):
        return pltpu.VMEM(shape, F32)

    half = [max(CUT[n][1], n - CUT[n][1]) for n in WIDE]
    quarter = [384 if n == 1536 else 256 for n in WIDE]
    scratch = [low(4, 4, CHIP, n) for n in WIDE] * 2
    scratch += [low(4, 2, CHIP, n) for n in half]
    scratch += [low(4, 4, CHIP, n) for n in half]
    scratch += [low(4, CHIP, n) for n in quarter]
    scratch += [low(4, CHIP, n) for n in half]
    scratch += [low(CHIP, n) for n in WIDE] * 2
    scratch += [wide(CHIP, n) for n in WIDE]
    scratch += [low(BLOCK, D)] * (4 * N_SUM)
    scratch += [wide(BLOCK, D)] * N_SUM
    scratch += [low(2, 32, ALL)] + [low(ROWS, D)] * 6 + [low(BLOCK, D)] * 3
    scratch += [low(ROWS, D)] * 5 + [wide(BLOCK, D)] * 10 + [wide(BLOCK, 1)] * 5
    scratch += [low(ROWS, 640)] * 3 + [wide(6, BLOCK, BLOCK)] * 3 + [low(ROWS, 256)] * 3
    scratch += [low(ROWS, 640)] * 3 + [wide(8, 640)] * 3
    scratch += [wide(ROWS, D)] * 2 + [low(ROWS, D)] * 4 + [wide(8, D)] * 4
    scratch += [wide(16, D), wide(16, D), wide(8, 640), wide(128, 128)]
    scratch += [pltpu.SemaphoreType.DMA((N_SEM,))] * 2 + [pltpu.SemaphoreType.DMA((1,))]
    vmem = pl.BlockSpec(memory_space=pltpu.VMEM)
    shapes = [
        jax.ShapeDtypeStruct((BLOCK, D), LOW),
        jax.ShapeDtypeStruct((BLOCK, D), F32),
        jax.ShapeDtypeStruct((BLOCK, D), LOW),
    ] + [jax.ShapeDtypeStruct((2, PIECE, n), F32) for n in WIDE]
    return pl.pallas_call(
        layers,
        out_shape=shapes,
        in_specs=[vmem] * 7,
        out_specs=[vmem] * len(shapes),
        scratch_shapes=scratch,
        compiler_params=pltpu.CompilerParams(
            collective_id=0, has_side_effects=True, vmem_limit_bytes=62 * 2**20
        ),
    )(pack, src_in, tgt_in, d_out, src_seg, tgt_seg, pick)


def selector():
    table = np.zeros((D, 128), np.float32)
    for chip in range(16):
        for i, row in enumerate((0, 1, 24, 25)):
            table[CHIP * chip + row, 4 * chip + i] = 1.0
    return table


def packed_shard(attn_in, attn_out, w_up, w_down, qv_bias, up_bias, gains, shifts):
    def attention(a):
        parts = jnp.concatenate([attn_in[a], attn_out[a].T[None]], axis=0)
        return parts.reshape(4, PIECE, 2, 192).transpose(2, 1, 0, 3).reshape(2, PIECE, 768)

    def feed(f):
        parts = jnp.stack([w_up[f], w_down[f].T])
        return parts.reshape(2, PIECE, 2, 768).transpose(2, 1, 0, 3).reshape(2, PIECE, 1536)

    across = jnp.concatenate([gains, shifts], axis=0).T
    across = jnp.broadcast_to(jnp.pad(across, ((0, 0), (0, 1)))[None], (2, PIECE, 16))
    query = qv_bias.reshape(3, 2, 2, 3, 2).transpose(2, 4, 0, 1, 3).reshape(2, 2, 18)
    up = up_bias.reshape(2, 2, 12, 2).transpose(1, 3, 0, 2).reshape(2, 2, 24)
    along = jnp.concatenate([query, up], axis=2)
    along = jnp.pad(along, ((0, 0), (0, PIECE - 2), (0, 112 - 42)))
    vectors = jnp.concatenate([across, along], axis=2)
    whole = jnp.concatenate(
        [attention(0), vectors, attention(1), feed(0), attention(2), feed(1)], axis=2
    )
    return jnp.pad(whole, ((0, 0), (0, 8), (0, 0)))


def local(
    src_in,
    tgt_in,
    src_seg,
    tgt_seg,
    attn_in,
    attn_out,
    w_up,
    w_down,
    qv_bias,
    up_bias,
    gains,
    shifts,
    d_out,
):
    pack = packed_shard(attn_in, attn_out, w_up, w_down, qv_bias, up_bias, gains, shifts)
    pick = jnp.asarray(selector(), LOW)
    dec_out, grad_src, grad_tgt, c0, c1, c2, c3, c4 = run_layers(
        pack, src_in, tgt_in, d_out, src_seg.reshape(64, 128), tgt_seg.reshape(64, 128), pick
    )
    att = jnp.stack([c0[:, :, :768], c1, c3]).reshape(3, 2, PIECE, 4, 192)
    ffn = jnp.stack([c2, c4]).reshape(2, 2, PIECE, 2, 768)
    grad_attn_in = att[:, :, :, :3].transpose(0, 3, 2, 1, 4).reshape(3, 3, PIECE, 384)
    grad_attn_out = att[:, :, :, 3].transpose(0, 1, 3, 2).reshape(3, 384, PIECE)
    grad_w_up = ffn[:, :, :, 0].transpose(0, 2, 1, 3).reshape(2, PIECE, 1536)
    grad_w_down = ffn[:, :, :, 1].transpose(0, 1, 3, 2).reshape(2, 1536, PIECE)
    vectors = c0[:, :, 768:]
    across = (vectors[0] + vectors[1])[:, :15].T
    along = vectors[:, :2, 16:58]
    query = along[:, :, :18].reshape(2, 2, 3, 2, 3).transpose(2, 3, 0, 4, 1).reshape(3, 2, 6, 2)
    up = along[:, :, 18:].reshape(2, 2, 2, 12).transpose(2, 0, 3, 1).reshape(2, 24, 2)
    return (
        dec_out,
        grad_src,
        grad_tgt.astype(F32),
        grad_attn_in,
        grad_attn_out,
        grad_w_up,
        grad_w_down,
        query,
        up,
        across[:5],
        across[5:],
    )


def solution(mesh):
    placed = (
        P(("section", "dp"), None),
        P(("section", "dp"), None),
        P(),
        P(),
        P(None, None, "section", "tensor"),
        P(None, "tensor", "section"),
        P(None, "section", "tensor"),
        P(None, "tensor", "section"),
        P(None, None, "tensor", "section"),
        P(None, "tensor", "section"),
        P(None, "section"),
        P(None, "section"),
        P(("section", "dp"), None),
    )
    return jax.shard_map(
        local,
        mesh=mesh,
        in_specs=placed,
        out_specs=(placed[0], placed[0], placed[0]) + placed[4:12],
        check_vma=False,
    )
```

```python
import jax
import jax.numpy as jnp
import numpy as np
from jax import lax
from jax.experimental import pallas as pl
from jax.experimental.pallas import tpu as pltpu
from jax.sharding import PartitionSpec as P

LOW = jnp.bfloat16
F32 = jnp.float32
MESH = pl.DeviceIdType.MESH
D = 768
HEAD = 64
BLOCK = 128
OWN = 64
ROWS = 2 * BLOCK
PIECE = 24
CHIP = 48
HEADS = 3
STEP = 32

WIDE = (896, 768, 1536, 768, 1536)
FROM = (0, 896, 1664, 3200, 3968)
ALL = 5504
CUT = {896: (256, 384, 640), 768: (256, 384, 640), 1536: (384, 768, 1152)}
ATT_CHUNK = (0, 1, 3)
FFN_CHUNK = (2, 4)
VEC_QV = 16
VEC_UP = 34
OUT_ROW = (10, 13, 11, 12, 14)
N_SUM = 11
N_SEM = 260


def nn(left, right):
    return jnp.dot(left, right, preferred_element_type=F32)


def nt(left, right):
    return lax.dot_general(left, right, (((1,), (1,)), ((), ())), preferred_element_type=F32)


def tn(left, right):
    return lax.dot_general(left, right, (((0,), (0,)), ((), ())), preferred_element_type=F32)


def normal_part(value):
    return 0.5 * (1.0 + lax.erf(value * 0.7071067811865476))


def layers(*refs):
    refs = list(refs)

    def take(count):
        part, refs[:] = refs[:count], refs[count:]
        return part

    attn_in, attn_out, w_up, w_down, qv_bias, up_bias, gains, shifts = take(8)
    src_in, tgt_in, d_out, src_seg, tgt_seg, pick = take(6)
    tokens, grads = take(2)
    w, g, r1, r2, q1, q2, dsnd, drcv, tot = [take(5) for _ in range(9)]
    snd1, rcv1, snd2, rcv2 = [take(N_SUM) for _ in range(4)]
    own = take(4)
    pack, both, src2, tgt2, h0, enc, h2, h3, dgot, dec_snd, tgt_snd, src_snd, grad_src = take(13)
    gl, gres, hat, rstd = [take(5) for _ in range(4)]
    qkv, prob, ctx, dqkv, bias = [take(3) for _ in range(5)]
    pre, act, dpre, up_row, up_sum = [take(2) for _ in range(5)]
    vec, side, bias_sum, flat = take(4)
    send_sem, recv_sem = take(2)

    me = lax.axis_index("section")
    z, y, c = me // 8, lax.rem(me // 2, 4), lax.rem(me, 2)
    chip = me // 2
    replica = lax.axis_index("dp")
    zp, zm, z2 = lax.rem(z + 1, 4), lax.rem(z + 3, 4), lax.rem(z + 2, 4)
    yp, ym, y2 = lax.rem(y + 1, 4), lax.rem(y + 3, 4), lax.rem(y + 2, 4)

    def at(zz, yy):
        return {"section": zz * 8 + yy * 2 + c}

    dzp, dzm, dyp, dym = at(zp, y), at(zm, y), at(z, yp), at(z, ym)
    twin = {"section": me + 1 - 2 * c}
    beside = {"tensor": 1 - lax.axis_index("tensor")}
    partner = {"dp": 1 - replica}
    behind = {"section": lax.rem(me + 29, 32)}
    ahead = {"section": lax.rem(me + 3, 32)}
    twin_behind = {"section": lax.rem(me + 1 - 2 * c + 29, 32)}
    other_ahead = {"section": lax.rem(me + 3, 32) + 2 * c - 1}
    my_block = pl.ds(pl.multiple_of(c * BLOCK, BLOCK), BLOCK)
    their_block = pl.ds(pl.multiple_of((1 - c) * BLOCK, BLOCK), BLOCK)
    mine = pl.multiple_of(c * OWN, OWN)
    theirs = pl.multiple_of((1 - c) * OWN, OWN)
    my_rows, their_rows = pl.ds(mine, OWN), pl.ds(theirs, OWN)
    part = lax.axis_index("tensor")

    barrier = pltpu.get_barrier_semaphore()
    greeted = (dzp, dzm, dyp, dym, twin, beside, partner)
    greeted += (behind, ahead, twin_behind, other_ahead)
    for device in greeted:
        pl.semaphore_signal(barrier, inc=1, device_id=device, device_id_type=MESH)

    def pack_attention(a):
        k = ATT_CHUNK[a]
        for half in range(2):
            cols = slice(half * 192, (half + 1) * 192)
            parts = [attn_in[a, m, :, cols] for m in range(3)] + [attn_out[a, :, cols]]
            pack[half, :PIECE, FROM[k] : FROM[k] + D] = jnp.concatenate(parts, axis=1)

    def pack_feed(f):
        k = FFN_CHUNK[f]
        for half in range(2):
            cols = slice(half * D, (half + 1) * D)
            pack[half, :PIECE, FROM[k] : FROM[k] + D] = w_up[f, :, cols]
            pack[half, :PIECE, FROM[k] + D : FROM[k] + 2 * D] = w_down[f, :, cols]

    def pack_vectors():
        across = jnp.concatenate([gains[...], shifts[...]], axis=0).astype(F32).T
        for half in range(2):
            pieces = [qv_bias[a, i, :, half * 3 : half * 3 + 3] for a in range(3) for i in range(2)]
            pieces += [up_bias[f, :, half * 12 : half * 12 + 12] for f in range(2)]
            along = jnp.concatenate([piece.astype(F32) for piece in pieces], axis=1)
            along = jnp.concatenate([along, jnp.zeros((PIECE - 2, 42), F32)], axis=0)
            blank = jnp.zeros((PIECE, 1), F32), jnp.zeros((PIECE, 70), F32)
            joined = jnp.concatenate([across, blank[0], along, blank[1]], axis=1)
            pack[half, :PIECE, D:896] = joined.astype(LOW)

    pack_attention(0)
    pack_vectors()
    pack_attention(1)
    pl.semaphore_wait(barrier, len(greeted))

    started = []

    def send(src, dst, device):
        index = len(started)
        copy = pltpu.make_async_remote_copy(
            src_ref=src,
            dst_ref=dst,
            send_sem=send_sem.at[index],
            recv_sem=recv_sem.at[index],
            device_id=device,
            device_id_type=MESH,
        )
        started.append(copy)
        copy.start()
        return copy

    def halves(k):
        a1, a2, b1 = CUT[WIDE[k]]
        n = WIDE[k]
        return (
            pl.ds(0, a2),
            pl.ds(a2, n - a2),
            pl.ds(0, a1),
            pl.ds(a1, a2 - a1),
            pl.ds(a2, b1 - a2),
            pl.ds(b1, n - b1),
        )

    lo, hi = pl.ds(0, 2), pl.ds(2, 2)
    first, second, third, fourth = {}, {}, {}, {}

    def gather0(k):
        a, b = halves(k)[:2]
        cols = slice(FROM[k], FROM[k] + WIDE[k])
        shard_copy[k].wait_recv()
        joined = jnp.concatenate(
            [both[0, :PIECE, cols].astype(F32), both[1, :PIECE, cols].astype(F32)], axis=0
        )
        w[k][z, y] = joined.astype(LOW)
        src_a, src_b = w[k].at[z, y, :, a], w[k].at[z, y, :, b]
        first[k] = [
            send(src_a, src_a, dzp),
            send(src_b, src_b, dyp),
            send(src_a, src_a, dzm),
            send(src_b, src_b, dym),
        ]

    def gather1(k):
        ap, am, bp, bm = halves(k)[2:]
        second[k] = []
        order = (
            (w[k].at[zm, y, :, ap], dzp),
            (w[k].at[z, ym, :, bp], dyp),
            (w[k].at[zp, y, :, am], dzm),
            (w[k].at[z, yp, :, bm], dym),
        )
        for copy, (block, device) in zip(first[k], order):
            copy.wait_recv()
            second[k].append(send(block, block, device))

    def gather2(k):
        a, b = halves(k)[:2]
        for copy in second[k]:
            copy.wait_recv()
        row, line = w[k].at[:, y, :, a], w[k].at[z, :, :, b]
        third[k] = [
            send(row, row, dyp),
            send(line, line, dzp),
            send(row, row, dym),
            send(line, line, dzm),
        ]

    def gather3(k):
        a, b = halves(k)[:2]
        fourth[k] = []
        order = (
            (w[k].at[lo, ym, :, a], dyp),
            (w[k].at[zm, lo, :, b], dzp),
            (w[k].at[hi, yp, :, a], dym),
            (w[k].at[zp, hi, :, b], dzm),
        )
        for copy, (block, device) in zip(third[k], order):
            copy.wait_recv()
            fourth[k].append(send(block, block, device))

    def gather4(k):
        for copy in fourth[k]:
            copy.wait_recv()

    def weight(k, start, stop):
        return w[k][:, :, :, start:stop].reshape(D, stop - start)

    down1, down2, down3, down4, down5, down6 = {}, {}, {}, {}, {}, {}

    def scatter0(k):
        a, b = halves(k)[:2]
        na, nb = pl.ds(0, a.size), pl.ds(0, b.size)
        down1[k] = [
            send(g[k].at[z2, lo, :, a], r1[k].at[0, :, :, na], dzp),
            send(g[k].at[lo, y2, :, b], r1[k].at[1, :, :, nb], dyp),
            send(g[k].at[z2, hi, :, a], r1[k].at[2, :, :, na], dzm),
            send(g[k].at[hi, y2, :, b], r1[k].at[3, :, :, nb], dym),
        ]

    def scatter1(k):
        a, b = halves(k)[:2]
        na, nb = pl.ds(0, a.size), pl.ds(0, b.size)
        copies, down2[k] = down1[k], []
        copies[0].wait_recv()
        g[k][zp, lo, :, a] += r1[k][0, :, :, na]
        down2[k].append(send(g[k].at[zp, :, :, a], r2[k].at[0, :, :, na], dzp))
        copies[1].wait_recv()
        g[k][lo, yp, :, b] += r1[k][1, :, :, nb]
        down2[k].append(send(g[k].at[:, yp, :, b], r2[k].at[1, :, :, nb], dyp))
        copies[2].wait_recv()
        g[k][zm, hi, :, a] += r1[k][2, :, :, na]
        down2[k].append(send(g[k].at[zm, :, :, a], r2[k].at[2, :, :, na], dzm))
        copies[3].wait_recv()
        g[k][hi, ym, :, b] += r1[k][3, :, :, nb]
        down2[k].append(send(g[k].at[:, ym, :, b], r2[k].at[3, :, :, nb], dym))

    def scatter2(k):
        a, b, ap, am, bp, bm = halves(k)
        na, nb = pl.ds(0, a.size), pl.ds(0, b.size)
        copies = down2[k]
        copies[0].wait_recv()
        copies[2].wait_recv()
        g[k][z, :, :, a] += r2[k][0, :, :, na] + r2[k][2, :, :, na]
        down3[k] = [
            send(g[k].at[z, y2, :, ap], q1[k].at[0, :, pl.ds(0, ap.size)], dyp),
            send(g[k].at[z, y2, :, am], q1[k].at[1, :, pl.ds(0, am.size)], dym),
        ]
        copies[1].wait_recv()
        copies[3].wait_recv()
        g[k][:, y, :, b] += r2[k][1, :, :, nb] + r2[k][3, :, :, nb]
        down3[k] += [
            send(g[k].at[z2, y, :, bp], q1[k].at[2, :, pl.ds(0, bp.size)], dzp),
            send(g[k].at[z2, y, :, bm], q1[k].at[3, :, pl.ds(0, bm.size)], dzm),
        ]

    def scatter3(k):
        a, b, ap, am, bp, bm = halves(k)
        na, nb = pl.ds(0, a.size), pl.ds(0, b.size)
        copies, down4[k] = down3[k], []
        copies[0].wait_recv()
        g[k][z, yp, :, ap] += q1[k][0, :, : ap.size]
        down4[k].append(send(g[k].at[z, yp, :, a], q2[k].at[0, :, na], dyp))
        copies[1].wait_recv()
        g[k][z, ym, :, am] += q1[k][1, :, : am.size]
        down4[k].append(send(g[k].at[z, ym, :, a], q2[k].at[1, :, na], dym))
        copies[2].wait_recv()
        g[k][zp, y, :, bp] += q1[k][2, :, : bp.size]
        down4[k].append(send(g[k].at[zp, y, :, b], q2[k].at[2, :, nb], dzp))
        copies[3].wait_recv()
        g[k][zm, y, :, bm] += q1[k][3, :, : bm.size]
        down4[k].append(send(g[k].at[zm, y, :, b], q2[k].at[3, :, nb], dzm))

    def scatter4(k):
        a, b = halves(k)[:2]
        for copy in down4[k]:
            copy.wait_recv()
        for cols, i in ((a, 0), (b, 2)):
            n = pl.ds(0, cols.size)
            got = q2[k][i, :, n].astype(F32) + q2[k][i + 1, :, n].astype(F32)
            dsnd[k][:, cols] = (g[k][z, y, :, cols].astype(F32) + got).astype(LOW)
        down5[k] = send(dsnd[k], drcv[k], partner)

    def scatter5(k):
        down5[k].wait_recv()
        tot[k][...] = dsnd[k][...].astype(F32) + drcv[k][...].astype(F32)
        rows_mine = pl.ds(pl.multiple_of(c * PIECE, PIECE), PIECE)
        rows_theirs = pl.ds(pl.multiple_of((1 - c) * PIECE, PIECE), PIECE)
        cols = pl.ds(FROM[k], WIDE[k])
        down6[k] = send(tot[k].at[rows_theirs], grads.at[c, :, cols], twin)
        grads[c, :, cols] = tot[k][rows_mine, :]

    def scatter6(k):
        down6[k].wait_recv()

    def put_grad(k, start, value):
        n = value.shape[1]
        g[k][:, :, :, start : start + n] = value.astype(LOW).reshape(4, 4, CHIP, n)

    hop1, hop2 = {}, {}

    def sum0(i, b, part):
        own[i % 4][b] = part
        snd1[i][b] = part.astype(LOW)
        hop1[i, b] = send(snd1[i].at[b, their_rows], rcv1[i].at[b], twin)

    def sum1(i, b):
        hop1[i, b].wait_recv()
        snd2[i][b] = (own[i % 4][b, my_rows, :] + rcv1[i][b].astype(F32)).astype(LOW)
        hop2[i, b] = send(snd2[i].at[b], rcv2[i].at[b], beside)

    def sum2(i, b):
        hop2[i, b].wait_recv()

    def summed(i, b, rows):
        return snd2[i][b, rows, :].astype(F32) + rcv2[i][b, rows, :].astype(F32)

    shared = {}

    def share(name, ref, b):
        view = ref.at[pl.ds(pl.multiple_of(b * BLOCK + mine, OWN), OWN)]
        shared[name, b] = send(view, view, twin)

    def share_wait(name, b):
        shared[name, b].wait_recv()

    def norm(i, n, b, x_ref, out_ref, name):
        sum2(i, b)
        gain, shift, out_shift = (vec[r : r + 1, :] for r in (n, 5 + n, OUT_ROW[n]))
        for r in range(0, OWN, STEP):
            rows = pl.ds(r, STEP)
            place = pl.ds(pl.multiple_of(b * BLOCK + mine + r, STEP), STEP)
            resid = x_ref[place, :].astype(F32) + (summed(i, b, rows) + out_shift)
            center = resid - jnp.mean(resid, axis=1, keepdims=True)
            spread = jnp.mean(center * center, axis=1, keepdims=True)
            scale = lax.rsqrt(spread + 1e-05)
            hat[n][b, rows, :] = center * scale
            rstd[n][b, rows, :] = scale
            result = (center * scale * gain + shift).astype(LOW)
            if name is None:
                out_ref[b, rows, :] = result.astype(F32)
            else:
                out_ref[place, :] = result
        if name is not None:
            share(name, out_ref, b)

    def norm_back(n, b, top):
        gain = vec[n : n + 1, :]
        sums = [jnp.zeros((8, D), F32) for _ in range(3)]
        for r in range(0, OWN, STEP):
            rows = pl.ds(r, STEP)
            place = pl.ds(pl.multiple_of(b * BLOCK + mine + r, STEP), STEP)
            grad = top(b, rows)
            x_hat = hat[n][b, rows, :]
            d_hat = grad * gain
            mean1 = jnp.mean(d_hat, axis=1, keepdims=True)
            mean2 = jnp.mean(d_hat * x_hat, axis=1, keepdims=True)
            resid = rstd[n][b, rows, :] * (d_hat - mean1 - x_hat * mean2)
            gres[n][b, rows, :] = resid
            gl[n][place, :] = resid.astype(LOW)
            for j, value in enumerate((grad * x_hat, grad, resid)):
                sums[j] = sums[j] + jnp.sum(value.reshape(STEP // 8, 8, D), axis=0)
        share(("gl", n), gl[n], b)
        for row, value in zip((n, 5 + n, OUT_ROW[n]), sums):
            side[b, row : row + 1, :] = jnp.sum(value, axis=0, keepdims=True)

    def lanes(start, width):
        return lax.broadcasted_iota(jnp.int32, (1, width), 1) + start

    def segment_row(table, shift, half):
        section = lax.rem(2 * chip + half + shift, 32)
        row = table[pl.ds(2 * section + replica, 1), :].astype(F32)
        return jnp.broadcast_to(row, (BLOCK, BLOCK))

    def allowed(a, half):
        query = segment_row(src_seg, 29, half) if a == 0 else segment_row(tgt_seg, 0, half)
        keys = segment_row(tgt_seg, 0, half) if a == 1 else segment_row(src_seg, 29, half)
        allow = query.T == keys
        if a == 1:
            row = lax.broadcasted_iota(jnp.int32, (BLOCK, BLOCK), 0)
            col = lax.broadcasted_iota(jnp.int32, (BLOCK, BLOCK), 1)
            allow = allow & (row >= col)
        return allow

    def heads_of(a, rows, head):
        return (qkv[a][rows, s + head * HEAD : s + (head + 1) * HEAD] for s in (0, 192, 384))

    def block(b):
        return slice(b * BLOCK, (b + 1) * BLOCK)

    def attend(a, b, x_ref, y_ref):
        k = ATT_CHUNK[a]
        rows = block(b)
        scale = jnp.where(lanes(0, 640) < 192, 0.125, 1.0)
        row_bias = bias[a][0:1, :]
        if a < 2:
            joined = nn(x_ref[rows, :], weight(k, 0, 640))
        else:
            left = nn(x_ref[rows, :], weight(k, 0, 256))
            right = nn(y_ref[rows, :], weight(k, 128, 640))
            middle = jnp.where(lanes(128, 128) < 192, left[:, 128:], right[:, :128])
            joined = jnp.concatenate([left[:, :128], middle, right[:, 128:]], axis=1)
        qkv[a][rows, :] = ((joined + row_bias) * scale).astype(LOW)
        allow = allowed(a, b)
        parts = [jnp.zeros((BLOCK, HEAD), LOW)]
        for head in range(HEADS):
            q, key, v = heads_of(a, rows, head)
            score = jnp.where(allow, nt(q, key), -1e30)
            expo = jnp.exp(score - jnp.max(score, axis=1, keepdims=True))
            p = expo / jnp.sum(expo, axis=1, keepdims=True)
            prob[a][b * HEADS + head] = p
            parts.append(nn(p.astype(LOW), v).astype(LOW))
        joined = jnp.concatenate(parts, axis=1)
        ctx[a][rows, :] = joined
        return nt(joined, weight(k, 512, 768))

    def attend_back(a, n, b):
        k = ATT_CHUNK[a]
        rows = block(b)
        d_ctx = nn(gl[n][rows, :], weight(k, 512, 768)).astype(LOW)
        d_q, d_k, d_v = [], [], []
        for head in range(HEADS):
            q, key, v = heads_of(a, rows, head)
            d_c = d_ctx[:, HEAD * (head + 1) : HEAD * (head + 2)]
            p = prob[a][b * HEADS + head]
            d_p = nt(d_c, v)
            delta = jnp.sum(p * d_p, axis=1, keepdims=True)
            d_s = (p * (d_p - delta)).astype(LOW)
            d_q.append((nn(d_s, key).astype(LOW).astype(F32) * 0.125).astype(LOW))
            d_k.append(tn(d_s, q).astype(LOW))
            d_v.append(tn(p.astype(LOW), d_c).astype(LOW))
        blank = jnp.zeros((BLOCK, HEAD), LOW)
        joined = jnp.concatenate(d_q + d_k + d_v + [blank], axis=1)
        dqkv[a][rows, :] = joined
        return joined

    def bias_sums(a):
        total = jnp.sum(dqkv[a][...].astype(F32).reshape(ROWS // 8, 8, 640), axis=0)
        bias_sum[a : a + 1, :] = jnp.sum(total, axis=0, keepdims=True)

    def query_part(value):
        return jnp.where(lanes(0, 256) < 192, value.astype(F32), 0.0).astype(LOW)

    def key_part(value, start):
        return jnp.where(lanes(start, value.shape[1]) < 192, 0.0, value.astype(F32)).astype(LOW)

    def self_back(a, n, b, i):
        sum0(i, b, nt(attend_back(a, n, b), weight(ATT_CHUNK[a], 0, 640)))

    def cross_back(b):
        joined = attend_back(2, 3, b)
        sum0(6, b, nt(key_part(joined[:, 128:], 128), weight(3, 128, 640)))
        sum0(7, b, nt(query_part(joined[:, :256]), weight(3, 0, 256)))

    def attend_weights(a, x_ref, y_ref):
        k = ATT_CHUNK[a]
        if a < 2:
            put_grad(k, 0, tn(x_ref[...], dqkv[a][:, 0:512]))
        else:
            left = tn(x_ref[...], query_part(dqkv[a][:, 0:256]))
            put_grad(k, 0, left + tn(y_ref[...], key_part(dqkv[a][:, 0:256], 0)))
            put_grad(k, 256, tn(y_ref[...], dqkv[a][:, 256:512]))

    def attend_weights_out(a, n, y_ref):
        k = ATT_CHUNK[a]
        tail = jnp.concatenate([dqkv[a][:, 512:640], jnp.zeros((ROWS, 128), LOW)], axis=1)
        put_grad(k, 512, tn(y_ref[...], tail) + tn(gl[n][...], ctx[a][...]))

    def feed(f, b, x_ref):
        k = FFN_CHUNK[f]
        pre[f][block(b), :] = nn(x_ref[block(b), :], weight(k, 0, D)) + up_row[f][0:1, :]

        @pl.loop(0, BLOCK // 16)
        def _(step):
            rows = pl.ds(pl.multiple_of(b * BLOCK + step * 16, 16), 16)
            value = pre[f][rows, :]
            act[f][rows, :] = (value * normal_part(value)).astype(LOW)

        return nt(act[f][block(b), :], weight(k, D, 2 * D))

    def feed_slope(f, b):
        @pl.loop(0, BLOCK // 16)
        def _(step):
            rows = pl.ds(pl.multiple_of(b * BLOCK + step * 16, 16), 16)
            value = pre[f][rows, :]
            bell = jnp.exp(-0.5 * value * value) * 0.3989422804014327
            pre[f][rows, :] = normal_part(value) + value * bell

    def feed_back(f, n, b):
        k = FFN_CHUNK[f]
        d_act = nn(gl[n][block(b), :], weight(k, D, 2 * D))
        d_pre = (pre[f][block(b), :] * d_act).astype(LOW)
        dpre[f][block(b), :] = d_pre
        return nt(d_pre, weight(k, 0, D))

    def feed_up_weights(f, x_ref):
        put_grad(FFN_CHUNK[f], 0, tn(x_ref[...], dpre[f][...]))

    def feed_down_weights(f, n):
        put_grad(FFN_CHUNK[f], D, tn(gl[n][...], act[f][...]))
        total = jnp.sum(dpre[f][...].astype(F32).reshape(ROWS // 8, 8, D), axis=0)
        up_sum[f][0:1, :] = jnp.sum(total, axis=0, keepdims=True)

    def unpack_vectors():
        packed = weight(0, D, 896)
        vec[...] = packed.astype(F32).T[:16, :]
        flat[...] = tn(packed, pick[...])
        for a in range(3):
            r = VEC_QV + 6 * a
            zero = jnp.zeros((1, HEAD), F32)
            pieces = [flat[r + i : r + i + 1, :HEAD] for i in range(6)]
            row = jnp.concatenate(pieces[:3] + [zero] * 3 + pieces[3:] + [zero], axis=1)
            bias[a][0:1, :] = row
        for f in range(2):
            r = VEC_UP + 12 * f
            pieces = [flat[r + i : r + i + 1, :HEAD] for i in range(12)]
            up_row[f][0:1, :] = jnp.concatenate(pieces, axis=1)

    def pack_vector_grads():
        rows = []
        for a in range(3):
            for s in (0, 384):
                rows += [bias_sum[a : a + 1, s + i * HEAD : s + (i + 1) * HEAD] for i in range(3)]
        for f in range(2):
            rows += [up_sum[f][0:1, i * HEAD : (i + 1) * HEAD] for i in range(12)]
        rows.append(jnp.zeros((6, HEAD), F32))
        small = jnp.concatenate(rows, axis=0).astype(LOW)
        spread = nt(small, pick[:, :HEAD])
        table = jnp.concatenate([side[0] + side[1], spread, jnp.zeros((64, D), F32)], axis=0)
        put_grad(0, D, table.T)

    shard_copy = {}

    def send_shard(k):
        cols = pl.ds(FROM[k], WIDE[k])
        shard_copy[k] = send(pack.at[1 - c, :, cols], both.at[c, :, cols], twin)
        both[c, :, FROM[k] : FROM[k] + WIDE[k]] = pack[c, :, FROM[k] : FROM[k] + WIDE[k]]

    send_shard(0)
    send_shard(1)
    half_rows = pl.ds(pl.multiple_of(part * OWN, OWN), OWN)
    landing = src2.at[pl.ds(pl.multiple_of((1 - c) * BLOCK + part * OWN, OWN), OWN)]
    landed = src2.at[pl.ds(pl.multiple_of(c * BLOCK + part * OWN, OWN), OWN)]
    src_copy = send(src_in.at[half_rows], landing, ahead)
    tgt_copy = send(tgt_in, tgt2.at[my_block], twin)
    d_out_copy = send(d_out.at[their_rows], dgot.at[c], twin)
    gather0(0)
    gather0(1)
    pack_feed(0)
    send_shard(2)
    pack_attention(2)
    send_shard(3)
    pack_feed(1)
    send_shard(4)
    tgt2[my_block, :] = tgt_in[...]
    dgot[c] = d_out[my_rows, :]
    side[...] = jnp.zeros((2, 16, D), F32)
    gather1(0)
    gather0(2)
    gather1(1)
    gather2(0)
    gather1(2)
    gather2(1)
    src_copy.wait_recv()
    src_half = send(landed, landed, beside)
    gather3(0)
    gather0(3)
    gather3(1)
    gather2(2)
    gather0(4)
    src_half.wait_recv()
    src_share = send(src2.at[my_block], src2.at[my_block], twin)

    gather4(0)
    unpack_vectors()
    src_share.wait_recv()
    sum0(0, 0, attend(0, 0, src2, src2))
    sum0(0, 1, attend(0, 1, src2, src2))
    sum1(0, 0)
    sum1(0, 1)
    gather1(3)
    gather1(4)
    gather2(3)
    gather4(1)
    tgt_copy.wait_recv()
    sum0(1, 0, attend(1, 0, tgt2, tgt2))
    norm(0, 0, 0, src2, h0, "h0")
    sum0(1, 1, attend(1, 1, tgt2, tgt2))
    sum1(1, 0)
    norm(0, 0, 1, src2, h0, "h0")
    sum1(1, 1)
    gather3(2)
    gather2(4)
    norm(1, 2, 0, tgt2, h2, "h2")
    norm(1, 2, 1, tgt2, h2, "h2")
    gather3(3)
    gather4(2)
    share_wait("h0", 0)
    sum0(2, 0, feed(0, 0, h0))
    share_wait("h0", 1)
    sum0(2, 1, feed(0, 1, h0))
    sum1(2, 0)
    sum1(2, 1)
    feed_slope(0, 0)
    feed_slope(0, 1)
    gather3(4)
    gather4(3)
    share_wait("h2", 0)
    share_wait("h2", 1)
    norm(2, 1, 0, h0, enc, "enc")
    share_wait("enc", 0)
    sum0(3, 0, attend(2, 0, h2, enc))
    norm(2, 1, 1, h0, enc, "enc")
    sum1(3, 0)
    share_wait("enc", 1)
    sum0(3, 1, attend(2, 1, h2, enc))
    sum1(3, 1)
    gather4(4)
    norm(3, 3, 0, h2, h3, "h3")
    share_wait("h3", 0)
    sum0(4, 0, feed(1, 0, h3))
    norm(3, 3, 1, h2, h3, "h3")
    sum1(4, 0)
    share_wait("h3", 1)
    sum0(4, 1, feed(1, 1, h3))
    sum1(4, 1)
    feed_slope(1, 0)
    feed_slope(1, 1)
    d_out_copy.wait_recv()

    def cotangent(b, rows):
        return dgot[b, rows, :].astype(F32)

    def rounded(n, i):
        def top(b, rows):
            return (gres[n][b, rows, :] + summed(i, b, rows)).astype(LOW).astype(F32)

        return top

    def from_cross(b, rows):
        return summed(6, b, rows).astype(LOW).astype(F32)

    norm(4, 4, 0, h3, dec_snd, None)
    norm_back(4, 0, cotangent)
    share_wait(("gl", 4), 0)
    sum0(5, 0, feed_back(1, 4, 0))
    norm(4, 4, 1, h3, dec_snd, None)
    norm_back(4, 1, cotangent)
    sum1(5, 0)
    share_wait(("gl", 4), 1)
    sum0(5, 1, feed_back(1, 4, 1))
    sum1(5, 1)
    feed_up_weights(1, h3)
    feed_down_weights(1, 4)
    scatter0(4)
    dec_copy = send(dec_snd.at[1 - c], tokens.at[0, my_rows], twin)
    tokens[0, my_rows, :] = dec_snd[c]
    sum2(5, 0)
    norm_back(3, 0, rounded(4, 5))
    share_wait(("gl", 3), 0)
    cross_back(0)
    sum2(5, 1)
    norm_back(3, 1, rounded(4, 5))
    sum1(6, 0)
    share_wait(("gl", 3), 1)
    cross_back(1)
    sum1(6, 1)
    sum1(7, 0)
    sum1(7, 1)
    scatter1(4)
    attend_weights(2, h2, enc)
    attend_weights_out(2, 3, enc)
    scatter0(3)
    sum2(6, 0)
    norm_back(1, 0, from_cross)
    share_wait(("gl", 1), 0)
    sum0(8, 0, feed_back(0, 1, 0))
    sum2(6, 1)
    norm_back(1, 1, from_cross)
    sum1(8, 0)
    share_wait(("gl", 1), 1)
    sum0(8, 1, feed_back(0, 1, 1))
    sum1(8, 1)
    scatter2(4)
    scatter1(3)
    feed_up_weights(0, h0)
    feed_down_weights(0, 1)
    scatter0(2)
    sum2(7, 0)
    norm_back(2, 0, rounded(3, 7))
    sum2(7, 1)
    norm_back(2, 1, rounded(3, 7))
    scatter3(4)
    share_wait(("gl", 2), 0)
    self_back(1, 2, 0, 9)
    sum2(8, 0)
    norm_back(0, 0, rounded(1, 8))
    share_wait(("gl", 2), 1)
    self_back(1, 2, 1, 9)
    sum2(8, 1)
    norm_back(0, 1, rounded(1, 8))
    attend_weights(1, tgt2, tgt2)
    attend_weights_out(1, 2, tgt2)
    scatter0(1)
    scatter1(2)
    scatter2(3)
    share_wait(("gl", 0), 0)
    self_back(0, 0, 0, 10)
    share_wait(("gl", 0), 1)
    self_back(0, 0, 1, 10)
    attend_weights(0, src2, src2)
    attend_weights_out(0, 0, src2)
    for a in range(3):
        bias_sums(a)
    pack_vector_grads()
    scatter0(0)
    sum1(10, 0)
    sum1(10, 1)
    sum1(9, 0)
    sum1(9, 1)
    scatter4(4)
    scatter3(3)
    scatter1(1)
    scatter1(0)
    scatter2(2)
    scatter4(3)
    piece_rows = pl.ds(pl.multiple_of(part * STEP, STEP), STEP)
    their_piece = pl.ds(pl.multiple_of(mine + part * STEP, STEP), STEP)
    for b in range(2):
        sum2(10, b)
        src_snd[b] = (gres[0][b] + summed(10, b, slice(None))).astype(LOW)
    src_back = send(src_snd.at[c, piece_rows], grad_src.at[their_piece], behind)
    src_back2 = send(src_snd.at[1 - c, piece_rows], grad_src.at[their_piece], twin_behind)
    for b in range(2):
        sum2(9, b)
        tgt_snd[b] = gres[2][b] + summed(9, b, slice(None))
    tgt_back = send(tgt_snd.at[1 - c], tokens.at[2, my_rows], twin)
    tokens[2, my_rows, :] = tgt_snd[c]
    scatter3(2)
    scatter2(1)
    scatter2(0)
    scatter4(2)
    scatter3(1)
    scatter3(0)
    scatter5(4)
    scatter5(3)
    scatter4(1)
    scatter4(0)
    scatter5(2)
    scatter5(1)
    scatter5(0)
    for k in (4, 3, 2, 1, 0):
        scatter6(k)
    src_back.wait_recv()
    src_back2.wait_recv()
    near = grad_src.at[pl.ds(pl.multiple_of(part * STEP, STEP), STEP)]
    far = grad_src.at[pl.ds(pl.multiple_of(part * STEP + OWN, STEP), STEP)]
    src_last = (send(near, near, beside), send(far, far, beside))
    for copy in (dec_copy, tgt_back) + src_last:
        copy.wait_recv()
    tokens[1] = grad_src[...].astype(F32)
    for copy in started:
        copy.wait_send()


def run_layers(*operands):
    def low(*shape):
        return pltpu.VMEM(shape, LOW)

    def wide(*shape):
        return pltpu.VMEM(shape, F32)

    half = [max(CUT[n][1], n - CUT[n][1]) for n in WIDE]
    quarter = [384 if n == 1536 else 256 for n in WIDE]
    scratch = [low(4, 4, CHIP, n) for n in WIDE] * 2
    scratch += [low(4, 2, CHIP, n) for n in half]
    scratch += [low(4, 4, CHIP, n) for n in half]
    scratch += [low(4, CHIP, n) for n in quarter]
    scratch += [low(4, CHIP, n) for n in half]
    scratch += [low(CHIP, n) for n in WIDE] * 2
    scratch += [wide(CHIP, n) for n in WIDE]
    scratch += [low(2, BLOCK, D)] * N_SUM + [low(2, OWN, D)] * (3 * N_SUM)
    scratch += [wide(2, BLOCK, D)] * 4
    scratch += [low(2, 32, ALL)] * 2 + [low(ROWS, D)] * 6 + [low(2, OWN, D)]
    scratch += [wide(2, OWN, D)] * 2 + [low(2, OWN, D), low(BLOCK, D)]
    scratch += [low(ROWS, D)] * 5 + [wide(2, OWN, D)] * 10 + [wide(2, OWN, 1)] * 5
    scratch += [low(ROWS, 640)] * 3 + [wide(6, BLOCK, BLOCK)] * 3 + [low(ROWS, 256)] * 3
    scratch += [low(ROWS, 640)] * 3 + [wide(8, 640)] * 3
    scratch += [wide(ROWS, D)] * 2 + [low(ROWS, D)] * 4 + [wide(8, D)] * 4
    scratch += [wide(16, D), wide(2, 16, D), wide(8, 640), wide(128, 128)]
    scratch += [pltpu.SemaphoreType.DMA((N_SEM,))] * 2
    vmem = pl.BlockSpec(memory_space=pltpu.VMEM)
    shapes = [
        jax.ShapeDtypeStruct((3, BLOCK, D), F32),
        jax.ShapeDtypeStruct((2, PIECE, ALL), F32),
    ]
    return pl.pallas_call(
        layers,
        out_shape=shapes,
        in_specs=[vmem] * len(operands),
        out_specs=[vmem] * len(shapes),
        scratch_shapes=scratch,
        compiler_params=pltpu.CompilerParams(
            collective_id=0, has_side_effects=True, vmem_limit_bytes=62 * 2**20
        ),
    )(*operands)


def selector():
    table = np.zeros((D, 128), np.float32)
    for chip in range(16):
        for i, row in enumerate((0, 1, 24, 25)):
            table[CHIP * chip + row, 4 * chip + i] = 1.0
    return table


def place_results(tokens_in, grads_in, *refs):
    outs, (tokens, grads, sem) = refs[:11], refs[11:]
    moves = [
        pltpu.make_async_copy(tokens_in, tokens, sem.at[0]),
        pltpu.make_async_copy(grads_in, grads, sem.at[1]),
    ]
    for move in moves:
        move.start()
    attn_in, attn_out, w_up, w_down, qv, up, gains, shifts = outs[3:]
    moves[0].wait()
    for i, out in enumerate(outs[:3]):
        out[...] = tokens[i].astype(out.dtype)
    moves[1].wait()
    for a in range(3):
        for m in range(4):
            col = FROM[ATT_CHUNK[a]] + m * 192
            joined = jnp.concatenate([grads[h, :, col : col + 192] for h in range(2)], axis=1)
            if m < 3:
                attn_in[a, m] = joined
            else:
                attn_out[a] = joined
    for f in range(2):
        col = FROM[FFN_CHUNK[f]]
        for half in range(2):
            w_up[f, :, half * D : (half + 1) * D] = grads[half, :, col : col + D]
            w_down[f, :, half * D : (half + 1) * D] = grads[half, :, col + D : col + 2 * D]
    across = (grads[0, :, D:896] + grads[1, :, D:896]).T
    gains[...] = across[:5]
    shifts[...] = across[5:15]
    for a in range(3):
        for i in range(2):
            col = D + VEC_QV + 6 * a + 3 * i
            qv[a, i] = jnp.concatenate([grads[h, 0:2, col : col + 3] for h in range(2)], axis=1)
    for f in range(2):
        col = D + VEC_UP + 12 * f
        up[f] = jnp.concatenate([grads[h, 0:2, col : col + 12] for h in range(2)], axis=1)


def placed_results(*results):
    vmem = pl.BlockSpec(memory_space=pltpu.VMEM)
    shapes = [
        jax.ShapeDtypeStruct((BLOCK, D), LOW),
        jax.ShapeDtypeStruct((BLOCK, D), F32),
        jax.ShapeDtypeStruct((BLOCK, D), F32),
        jax.ShapeDtypeStruct((3, 3, PIECE, 384), F32),
        jax.ShapeDtypeStruct((3, PIECE, 384), F32),
        jax.ShapeDtypeStruct((2, PIECE, 1536), F32),
        jax.ShapeDtypeStruct((2, PIECE, 1536), F32),
        jax.ShapeDtypeStruct((3, 2, 2, 6), F32),
        jax.ShapeDtypeStruct((2, 2, 24), F32),
        jax.ShapeDtypeStruct((5, PIECE), F32),
        jax.ShapeDtypeStruct((10, PIECE), F32),
    ]
    return pl.pallas_call(
        place_results,
        out_shape=shapes,
        in_specs=[pl.BlockSpec(memory_space=pltpu.HBM)] * len(results),
        out_specs=[vmem] * len(shapes),
        scratch_shapes=[pltpu.VMEM(r.shape, r.dtype) for r in results]
        + [pltpu.SemaphoreType.DMA((len(results),))],
        compiler_params=pltpu.CompilerParams(vmem_limit_bytes=32 * 2**20),
    )(*results)


def local(
    src_in,
    tgt_in,
    src_seg,
    tgt_seg,
    attn_in,
    attn_out,
    w_up,
    w_down,
    qv_bias,
    up_bias,
    gains,
    shifts,
    d_out,
):
    pick = jnp.asarray(selector(), LOW)
    results = run_layers(
        attn_in,
        attn_out.transpose(0, 2, 1),
        w_up,
        w_down.transpose(0, 2, 1),
        qv_bias.transpose(0, 1, 3, 2),
        up_bias.transpose(0, 2, 1),
        gains,
        shifts,
        src_in,
        tgt_in,
        d_out,
        src_seg.reshape(64, 128),
        tgt_seg.reshape(64, 128),
        pick,
    )
    dec, src, tgt, att_in, att_out, up, down, qv, up_vec, gain, shift = placed_results(*results)
    return (
        dec,
        src,
        tgt,
        att_in,
        att_out.transpose(0, 2, 1),
        up,
        down.transpose(0, 2, 1),
        qv.transpose(0, 1, 3, 2),
        up_vec.transpose(0, 2, 1),
        gain,
        shift,
    )


def solution(mesh):
    placed = (
        P(("section", "dp"), None),
        P(("section", "dp"), None),
        P(),
        P(),
        P(None, None, "section", "tensor"),
        P(None, "tensor", "section"),
        P(None, "section", "tensor"),
        P(None, "tensor", "section"),
        P(None, None, "tensor", "section"),
        P(None, "tensor", "section"),
        P(None, "section"),
        P(None, "section"),
        P(("section", "dp"), None),
    )
    return jax.shard_map(
        local,
        mesh=mesh,
        in_specs=placed,
        out_specs=(placed[0], placed[0], placed[0]) + placed[4:12],
        check_vma=False,
    )
```

```python
import jax
import jax.numpy as jnp
import numpy as np
from jax import lax
from jax.experimental import pallas as pl
from jax.experimental.pallas import tpu as pltpu
from jax.sharding import PartitionSpec as P

LOW = jnp.bfloat16
F32 = jnp.float32
MESH = pl.DeviceIdType.MESH
D = 768
HEAD = 64
BLOCK = 128
OWN = 64
ROWS = 2 * BLOCK
PIECE = 24
CHIP = 48
HEADS = 3
STEP = 32

WIDE = (896, 768, 1536, 768, 1536)
FROM = (0, 896, 1664, 3200, 3968)
ALL = 5504
CUT = {896: (256, 384, 640), 768: (256, 384, 640), 1536: (384, 768, 1152)}
ATT_CHUNK = (0, 1, 3)
FFN_CHUNK = (2, 4)
VEC_QV = 16
VEC_UP = 34
OUT_ROW = (10, 13, 11, 12, 14)
N_SUM = 11
N_SEM = 260


def nn(left, right):
    return jnp.dot(left, right, preferred_element_type=F32)


def nt(left, right):
    return lax.dot_general(left, right, (((1,), (1,)), ((), ())), preferred_element_type=F32)


def tn(left, right):
    return lax.dot_general(left, right, (((0,), (0,)), ((), ())), preferred_element_type=F32)


def normal_part(value):
    return 0.5 * (1.0 + lax.erf(value * 0.7071067811865476))


def layers(*refs):
    refs = list(refs)

    def take(count):
        part, refs[:] = refs[:count], refs[count:]
        return part

    attn_in, attn_out, w_up, w_down, qv_bias, up_bias, gains, shifts = take(8)
    src_in, tgt_in, d_out, src_seg, tgt_seg, pick = take(6)
    tokens, grads = take(2)
    w, g, r1, r2, q1, q2, dsnd, drcv, tot = [take(5) for _ in range(9)]
    snd1, rcv1, snd2, rcv2 = [take(N_SUM) for _ in range(4)]
    own = take(4)
    pack, both, src2, tgt2, h0, enc, h2, h3, dgot, dec_snd, tgt_snd, src_snd, grad_src = take(13)
    gl, gres, hat, rstd = [take(5) for _ in range(4)]
    qkv, prob, ctx, dqkv, bias = [take(3) for _ in range(5)]
    pre, act, dpre, up_row, up_sum = [take(2) for _ in range(5)]
    vec, side, bias_sum, flat = take(4)
    send_sem, recv_sem = take(2)

    me = lax.axis_index("section")
    z, y, c = me // 8, lax.rem(me // 2, 4), lax.rem(me, 2)
    chip = me // 2
    replica = lax.axis_index("dp")
    zp, zm, z2 = lax.rem(z + 1, 4), lax.rem(z + 3, 4), lax.rem(z + 2, 4)
    yp, ym, y2 = lax.rem(y + 1, 4), lax.rem(y + 3, 4), lax.rem(y + 2, 4)

    def at(zz, yy):
        return {"section": zz * 8 + yy * 2 + c}

    dzp, dzm, dyp, dym = at(zp, y), at(zm, y), at(z, yp), at(z, ym)
    twin = {"section": me + 1 - 2 * c}
    beside = {"tensor": 1 - lax.axis_index("tensor")}
    partner = {"dp": 1 - replica}
    behind = {"section": lax.rem(me + 29, 32)}
    ahead = {"section": lax.rem(me + 3, 32)}
    twin_behind = {"section": lax.rem(me + 1 - 2 * c + 29, 32)}
    other_ahead = {"section": lax.rem(me + 3, 32) + 2 * c - 1}
    my_block = pl.ds(pl.multiple_of(c * BLOCK, BLOCK), BLOCK)
    their_block = pl.ds(pl.multiple_of((1 - c) * BLOCK, BLOCK), BLOCK)
    mine = pl.multiple_of(c * OWN, OWN)
    theirs = pl.multiple_of((1 - c) * OWN, OWN)
    my_rows, their_rows = pl.ds(mine, OWN), pl.ds(theirs, OWN)
    part = lax.axis_index("tensor")

    barrier = pltpu.get_barrier_semaphore()
    greeted = (dzp, dzm, dyp, dym, twin, beside, partner)
    greeted += (behind, ahead, twin_behind, other_ahead)
    for device in greeted:
        pl.semaphore_signal(barrier, inc=1, device_id=device, device_id_type=MESH)

    def pack_attention(a):
        k = ATT_CHUNK[a]
        for half in range(2):
            cols = slice(half * 192, (half + 1) * 192)
            parts = [attn_in[a, m, :, cols] for m in range(3)] + [attn_out[a, :, cols]]
            pack[half, :PIECE, FROM[k] : FROM[k] + D] = jnp.concatenate(parts, axis=1)

    def pack_feed(f):
        k = FFN_CHUNK[f]
        for half in range(2):
            cols = slice(half * D, (half + 1) * D)
            pack[half, :PIECE, FROM[k] : FROM[k] + D] = w_up[f, :, cols]
            pack[half, :PIECE, FROM[k] + D : FROM[k] + 2 * D] = w_down[f, :, cols]

    def pack_vectors():
        across = jnp.concatenate([gains[...], shifts[...]], axis=0).astype(F32).T
        for half in range(2):
            pieces = [qv_bias[a, i, :, half * 3 : half * 3 + 3] for a in range(3) for i in range(2)]
            pieces += [up_bias[f, :, half * 12 : half * 12 + 12] for f in range(2)]
            along = jnp.concatenate([piece.astype(F32) for piece in pieces], axis=1)
            along = jnp.concatenate([along, jnp.zeros((PIECE - 2, 42), F32)], axis=0)
            blank = jnp.zeros((PIECE, 1), F32), jnp.zeros((PIECE, 70), F32)
            joined = jnp.concatenate([across, blank[0], along, blank[1]], axis=1)
            pack[half, :PIECE, D:896] = joined.astype(LOW)

    pack_attention(0)
    pack_vectors()
    pack_attention(1)
    pl.semaphore_wait(barrier, len(greeted))

    started = []

    def send(src, dst, device):
        index = len(started)
        copy = pltpu.make_async_remote_copy(
            src_ref=src,
            dst_ref=dst,
            send_sem=send_sem.at[index],
            recv_sem=recv_sem.at[index],
            device_id=device,
            device_id_type=MESH,
        )
        started.append(copy)
        copy.start()
        return copy

    def halves(k):
        a1, a2, b1 = CUT[WIDE[k]]
        n = WIDE[k]
        return (
            pl.ds(0, a2),
            pl.ds(a2, n - a2),
            pl.ds(0, a1),
            pl.ds(a1, a2 - a1),
            pl.ds(a2, b1 - a2),
            pl.ds(b1, n - b1),
        )

    lo, hi = pl.ds(0, 2), pl.ds(2, 2)
    first, second, third, fourth = {}, {}, {}, {}

    def gather0(k):
        a, b = halves(k)[:2]
        cols = slice(FROM[k], FROM[k] + WIDE[k])
        shard_copy[k].wait_recv()
        joined = jnp.concatenate(
            [both[0, :PIECE, cols].astype(F32), both[1, :PIECE, cols].astype(F32)], axis=0
        )
        w[k][z, y] = joined.astype(LOW)
        src_a, src_b = w[k].at[z, y, :, a], w[k].at[z, y, :, b]
        first[k] = [
            send(src_a, src_a, dzp),
            send(src_b, src_b, dyp),
            send(src_a, src_a, dzm),
            send(src_b, src_b, dym),
        ]

    def gather1(k):
        ap, am, bp, bm = halves(k)[2:]
        second[k] = []
        order = (
            (w[k].at[zm, y, :, ap], dzp),
            (w[k].at[z, ym, :, bp], dyp),
            (w[k].at[zp, y, :, am], dzm),
            (w[k].at[z, yp, :, bm], dym),
        )
        for copy, (block, device) in zip(first[k], order):
            copy.wait_recv()
            second[k].append(send(block, block, device))

    def gather2(k):
        a, b = halves(k)[:2]
        for copy in second[k]:
            copy.wait_recv()
        row, line = w[k].at[:, y, :, a], w[k].at[z, :, :, b]
        third[k] = [
            send(row, row, dyp),
            send(line, line, dzp),
            send(row, row, dym),
            send(line, line, dzm),
        ]

    def gather3(k):
        a, b = halves(k)[:2]
        fourth[k] = []
        order = (
            (w[k].at[lo, ym, :, a], dyp),
            (w[k].at[zm, lo, :, b], dzp),
            (w[k].at[hi, yp, :, a], dym),
            (w[k].at[zp, hi, :, b], dzm),
        )
        for copy, (block, device) in zip(third[k], order):
            copy.wait_recv()
            fourth[k].append(send(block, block, device))

    def gather4(k):
        for copy in fourth[k]:
            copy.wait_recv()

    def weight(k, start, stop):
        return w[k][:, :, :, start:stop].reshape(D, stop - start)

    down1, down2, down3, down4, down5, down6 = {}, {}, {}, {}, {}, {}

    def scatter0(k, half=None):
        a, b = halves(k)[:2]
        na, nb = pl.ds(0, a.size), pl.ds(0, b.size)
        copies = down1.setdefault(k, {})
        if half != 1:
            copies[0] = send(g[k].at[z2, lo, :, a], r1[k].at[0, :, :, na], dzp)
            copies[2] = send(g[k].at[z2, hi, :, a], r1[k].at[2, :, :, na], dzm)
        if half != 0:
            copies[1] = send(g[k].at[lo, y2, :, b], r1[k].at[1, :, :, nb], dyp)
            copies[3] = send(g[k].at[hi, y2, :, b], r1[k].at[3, :, :, nb], dym)

    def scatter1(k):
        a, b = halves(k)[:2]
        na, nb = pl.ds(0, a.size), pl.ds(0, b.size)
        copies, down2[k] = down1[k], []
        copies[0].wait_recv()
        g[k][zp, lo, :, a] += r1[k][0, :, :, na]
        down2[k].append(send(g[k].at[zp, :, :, a], r2[k].at[0, :, :, na], dzp))
        copies[1].wait_recv()
        g[k][lo, yp, :, b] += r1[k][1, :, :, nb]
        down2[k].append(send(g[k].at[:, yp, :, b], r2[k].at[1, :, :, nb], dyp))
        copies[2].wait_recv()
        g[k][zm, hi, :, a] += r1[k][2, :, :, na]
        down2[k].append(send(g[k].at[zm, :, :, a], r2[k].at[2, :, :, na], dzm))
        copies[3].wait_recv()
        g[k][hi, ym, :, b] += r1[k][3, :, :, nb]
        down2[k].append(send(g[k].at[:, ym, :, b], r2[k].at[3, :, :, nb], dym))

    def scatter2(k):
        a, b, ap, am, bp, bm = halves(k)
        na, nb = pl.ds(0, a.size), pl.ds(0, b.size)
        copies = down2[k]
        copies[0].wait_recv()
        copies[2].wait_recv()
        g[k][z, :, :, a] += r2[k][0, :, :, na] + r2[k][2, :, :, na]
        down3[k] = [
            send(g[k].at[z, y2, :, ap], q1[k].at[0, :, pl.ds(0, ap.size)], dyp),
            send(g[k].at[z, y2, :, am], q1[k].at[1, :, pl.ds(0, am.size)], dym),
        ]
        copies[1].wait_recv()
        copies[3].wait_recv()
        g[k][:, y, :, b] += r2[k][1, :, :, nb] + r2[k][3, :, :, nb]
        down3[k] += [
            send(g[k].at[z2, y, :, bp], q1[k].at[2, :, pl.ds(0, bp.size)], dzp),
            send(g[k].at[z2, y, :, bm], q1[k].at[3, :, pl.ds(0, bm.size)], dzm),
        ]

    def scatter3(k):
        a, b, ap, am, bp, bm = halves(k)
        na, nb = pl.ds(0, a.size), pl.ds(0, b.size)
        copies, down4[k] = down3[k], []
        copies[0].wait_recv()
        g[k][z, yp, :, ap] += q1[k][0, :, : ap.size]
        down4[k].append(send(g[k].at[z, yp, :, a], q2[k].at[0, :, na], dyp))
        copies[1].wait_recv()
        g[k][z, ym, :, am] += q1[k][1, :, : am.size]
        down4[k].append(send(g[k].at[z, ym, :, a], q2[k].at[1, :, na], dym))
        copies[2].wait_recv()
        g[k][zp, y, :, bp] += q1[k][2, :, : bp.size]
        down4[k].append(send(g[k].at[zp, y, :, b], q2[k].at[2, :, nb], dzp))
        copies[3].wait_recv()
        g[k][zm, y, :, bm] += q1[k][3, :, : bm.size]
        down4[k].append(send(g[k].at[zm, y, :, b], q2[k].at[3, :, nb], dzm))

    def scatter4(k):
        a, b = halves(k)[:2]
        for copy in down4[k]:
            copy.wait_recv()
        for cols, i in ((a, 0), (b, 2)):
            n = pl.ds(0, cols.size)
            got = q2[k][i, :, n].astype(F32) + q2[k][i + 1, :, n].astype(F32)
            dsnd[k][:, cols] = (g[k][z, y, :, cols].astype(F32) + got).astype(LOW)
        down5[k] = send(dsnd[k], drcv[k], partner)

    def scatter5(k):
        down5[k].wait_recv()
        tot[k][...] = dsnd[k][...].astype(F32) + drcv[k][...].astype(F32)
        rows_mine = pl.ds(pl.multiple_of(c * PIECE, PIECE), PIECE)
        rows_theirs = pl.ds(pl.multiple_of((1 - c) * PIECE, PIECE), PIECE)
        cols = pl.ds(FROM[k], WIDE[k])
        down6[k] = send(tot[k].at[rows_theirs], grads.at[c, :, cols], twin)
        grads[c, :, cols] = tot[k][rows_mine, :]

    def scatter6(k):
        down6[k].wait_recv()

    def put_grad(k, start, value):
        n = value.shape[1]
        g[k][:, :, :, start : start + n] = value.astype(LOW).reshape(4, 4, CHIP, n)

    hop1, hop2 = {}, {}

    def sum0(i, b, part):
        own[i % 4][b] = part
        snd1[i][b] = part.astype(LOW)
        hop1[i, b] = send(snd1[i].at[b, their_rows], rcv1[i].at[b], twin)

    def sum1(i, b):
        hop1[i, b].wait_recv()
        snd2[i][b] = (own[i % 4][b, my_rows, :] + rcv1[i][b].astype(F32)).astype(LOW)
        hop2[i, b] = send(snd2[i].at[b], rcv2[i].at[b], beside)

    def sum2(i, b):
        hop2[i, b].wait_recv()

    def summed(i, b, rows):
        return snd2[i][b, rows, :].astype(F32) + rcv2[i][b, rows, :].astype(F32)

    shared = {}

    def share(name, ref, b):
        view = ref.at[pl.ds(pl.multiple_of(b * BLOCK + mine, OWN), OWN)]
        shared[name, b] = send(view, view, twin)

    def share_wait(name, b):
        shared[name, b].wait_recv()

    def norm(i, n, b, x_ref, out_ref, name):
        sum2(i, b)
        gain, shift, out_shift = (vec[r : r + 1, :] for r in (n, 5 + n, OUT_ROW[n]))
        for r in range(0, OWN, STEP):
            rows = pl.ds(r, STEP)
            place = pl.ds(pl.multiple_of(b * BLOCK + mine + r, STEP), STEP)
            resid = x_ref[place, :].astype(F32) + (summed(i, b, rows) + out_shift)
            center = resid - jnp.mean(resid, axis=1, keepdims=True)
            spread = jnp.mean(center * center, axis=1, keepdims=True)
            scale = lax.rsqrt(spread + 1e-05)
            hat[n][b, rows, :] = center * scale
            rstd[n][b, rows, :] = scale
            result = (center * scale * gain + shift).astype(LOW)
            if name is None:
                out_ref[b, rows, :] = result
            else:
                out_ref[place, :] = result
        if name is not None:
            share(name, out_ref, b)

    def norm_back(n, b, top):
        gain = vec[n : n + 1, :]
        sums = [jnp.zeros((8, D), F32) for _ in range(3)]
        for r in range(0, OWN, STEP):
            rows = pl.ds(r, STEP)
            place = pl.ds(pl.multiple_of(b * BLOCK + mine + r, STEP), STEP)
            grad = top(b, rows)
            x_hat = hat[n][b, rows, :]
            d_hat = grad * gain
            mean1 = jnp.mean(d_hat, axis=1, keepdims=True)
            mean2 = jnp.mean(d_hat * x_hat, axis=1, keepdims=True)
            resid = rstd[n][b, rows, :] * (d_hat - mean1 - x_hat * mean2)
            gres[n][b, rows, :] = resid
            gl[n][place, :] = resid.astype(LOW)
            for j, value in enumerate((grad * x_hat, grad, resid)):
                sums[j] = sums[j] + jnp.sum(value.reshape(STEP // 8, 8, D), axis=0)
        share(("gl", n), gl[n], b)
        for row, value in zip((n, 5 + n, OUT_ROW[n]), sums):
            side[b, row : row + 1, :] = jnp.sum(value, axis=0, keepdims=True)

    def lanes(start, width):
        return lax.broadcasted_iota(jnp.int32, (1, width), 1) + start

    def segment_row(table, shift, half):
        section = lax.rem(2 * chip + half + shift, 32)
        row = table[pl.ds(2 * section + replica, 1), :].astype(F32)
        return jnp.broadcast_to(row, (BLOCK, BLOCK))

    def allowed(a, half):
        query = segment_row(src_seg, 29, half) if a == 0 else segment_row(tgt_seg, 0, half)
        keys = segment_row(tgt_seg, 0, half) if a == 1 else segment_row(src_seg, 29, half)
        allow = query.T == keys
        if a == 1:
            row = lax.broadcasted_iota(jnp.int32, (BLOCK, BLOCK), 0)
            col = lax.broadcasted_iota(jnp.int32, (BLOCK, BLOCK), 1)
            allow = allow & (row >= col)
        return allow

    def heads_of(a, rows, head):
        return (qkv[a][rows, s + head * HEAD : s + (head + 1) * HEAD] for s in (0, 192, 384))

    def block(b):
        return slice(b * BLOCK, (b + 1) * BLOCK)

    def attend(a, b, x_ref, y_ref):
        k = ATT_CHUNK[a]
        rows = block(b)
        scale = jnp.where(lanes(0, 640) < 192, 0.125, 1.0)
        row_bias = bias[a][0:1, :]
        if a < 2:
            joined = nn(x_ref[rows, :], weight(k, 0, 640))
        else:
            left = nn(x_ref[rows, :], weight(k, 0, 256))
            right = nn(y_ref[rows, :], weight(k, 128, 640))
            middle = jnp.where(lanes(128, 128) < 192, left[:, 128:], right[:, :128])
            joined = jnp.concatenate([left[:, :128], middle, right[:, 128:]], axis=1)
        qkv[a][rows, :] = ((joined + row_bias) * scale).astype(LOW)
        allow = allowed(a, b)
        parts = [jnp.zeros((BLOCK, HEAD), LOW)]
        for head in range(HEADS):
            q, key, v = heads_of(a, rows, head)
            score = jnp.where(allow, nt(q, key), -1e30)
            expo = jnp.exp(score - jnp.max(score, axis=1, keepdims=True))
            p = expo / jnp.sum(expo, axis=1, keepdims=True)
            prob[a][b * HEADS + head] = p
            parts.append(nn(p.astype(LOW), v).astype(LOW))
        joined = jnp.concatenate(parts, axis=1)
        ctx[a][rows, :] = joined
        return nt(joined, weight(k, 512, 768))

    def attend_back(a, n, b):
        k = ATT_CHUNK[a]
        rows = block(b)
        d_ctx = nn(gl[n][rows, :], weight(k, 512, 768)).astype(LOW)
        d_q, d_k, d_v = [], [], []
        for head in range(HEADS):
            q, key, v = heads_of(a, rows, head)
            d_c = d_ctx[:, HEAD * (head + 1) : HEAD * (head + 2)]
            p = prob[a][b * HEADS + head]
            d_p = nt(d_c, v)
            delta = jnp.sum(p * d_p, axis=1, keepdims=True)
            d_s = (p * (d_p - delta)).astype(LOW)
            d_q.append((nn(d_s, key).astype(LOW).astype(F32) * 0.125).astype(LOW))
            d_k.append(tn(d_s, q).astype(LOW))
            d_v.append(tn(p.astype(LOW), d_c).astype(LOW))
        blank = jnp.zeros((BLOCK, HEAD), LOW)
        joined = jnp.concatenate(d_q + d_k + d_v + [blank], axis=1)
        dqkv[a][rows, :] = joined
        return joined

    def bias_sums(a):
        total = jnp.sum(dqkv[a][...].astype(F32).reshape(ROWS // 8, 8, 640), axis=0)
        bias_sum[a : a + 1, :] = jnp.sum(total, axis=0, keepdims=True)

    def query_part(value):
        return jnp.where(lanes(0, 256) < 192, value.astype(F32), 0.0).astype(LOW)

    def key_part(value, start):
        return jnp.where(lanes(start, value.shape[1]) < 192, 0.0, value.astype(F32)).astype(LOW)

    def self_back(a, n, b, i):
        sum0(i, b, nt(attend_back(a, n, b), weight(ATT_CHUNK[a], 0, 640)))

    def cross_back(b):
        joined = attend_back(2, 3, b)
        sum0(6, b, nt(key_part(joined[:, 128:], 128), weight(3, 128, 640)))
        sum0(7, b, nt(query_part(joined[:, :256]), weight(3, 0, 256)))

    def attend_weights(a, x_ref, y_ref):
        k = ATT_CHUNK[a]
        if a < 2:
            put_grad(k, 0, tn(x_ref[...], dqkv[a][:, 0:512]))
        else:
            left = tn(x_ref[...], query_part(dqkv[a][:, 0:256]))
            put_grad(k, 0, left + tn(y_ref[...], key_part(dqkv[a][:, 0:256], 0)))
            put_grad(k, 256, tn(y_ref[...], dqkv[a][:, 256:512]))

    def attend_weights_out(a, n, y_ref):
        k = ATT_CHUNK[a]
        tail = jnp.concatenate([dqkv[a][:, 512:640], jnp.zeros((ROWS, 128), LOW)], axis=1)
        put_grad(k, 512, tn(y_ref[...], tail) + tn(gl[n][...], ctx[a][...]))

    def feed(f, b, x_ref):
        k = FFN_CHUNK[f]
        pre[f][block(b), :] = nn(x_ref[block(b), :], weight(k, 0, D)) + up_row[f][0:1, :]

        @pl.loop(0, BLOCK // 16)
        def _(step):
            rows = pl.ds(pl.multiple_of(b * BLOCK + step * 16, 16), 16)
            value = pre[f][rows, :]
            act[f][rows, :] = (value * normal_part(value)).astype(LOW)

        return nt(act[f][block(b), :], weight(k, D, 2 * D))

    def feed_slope(f, b):
        @pl.loop(0, BLOCK // 16)
        def _(step):
            rows = pl.ds(pl.multiple_of(b * BLOCK + step * 16, 16), 16)
            value = pre[f][rows, :]
            bell = jnp.exp(-0.5 * value * value) * 0.3989422804014327
            pre[f][rows, :] = normal_part(value) + value * bell

    def feed_back(f, n, b):
        k = FFN_CHUNK[f]
        d_act = nn(gl[n][block(b), :], weight(k, D, 2 * D))
        d_pre = (pre[f][block(b), :] * d_act).astype(LOW)
        dpre[f][block(b), :] = d_pre
        return nt(d_pre, weight(k, 0, D))

    def feed_up_weights(f, x_ref):
        put_grad(FFN_CHUNK[f], 0, tn(x_ref[...], dpre[f][...]))

    def up_sums(f):
        total = jnp.sum(dpre[f][...].astype(F32).reshape(ROWS // 8, 8, D), axis=0)
        up_sum[f][0:1, :] = jnp.sum(total, axis=0, keepdims=True)

    def feed_down_weights(f, n):
        put_grad(FFN_CHUNK[f], D, tn(gl[n][...], act[f][...]))

    def unpack_vectors():
        packed = weight(0, D, 896)
        vec[...] = packed.astype(F32).T[:16, :]
        flat[...] = tn(packed, pick[...])
        for a in range(3):
            r = VEC_QV + 6 * a
            zero = jnp.zeros((1, HEAD), F32)
            pieces = [flat[r + i : r + i + 1, :HEAD] for i in range(6)]
            row = jnp.concatenate(pieces[:3] + [zero] * 3 + pieces[3:] + [zero], axis=1)
            bias[a][0:1, :] = row
        for f in range(2):
            r = VEC_UP + 12 * f
            pieces = [flat[r + i : r + i + 1, :HEAD] for i in range(12)]
            up_row[f][0:1, :] = jnp.concatenate(pieces, axis=1)

    def pack_vector_grads():
        rows = []
        for a in range(3):
            for s in (0, 384):
                rows += [bias_sum[a : a + 1, s + i * HEAD : s + (i + 1) * HEAD] for i in range(3)]
        for f in range(2):
            rows += [up_sum[f][0:1, i * HEAD : (i + 1) * HEAD] for i in range(12)]
        rows.append(jnp.zeros((6, HEAD), F32))
        small = jnp.concatenate(rows, axis=0).astype(LOW)
        spread = nt(small, pick[:, :HEAD])
        table = jnp.concatenate([side[0] + side[1], spread, jnp.zeros((64, D), F32)], axis=0)
        put_grad(0, D, table.T)

    shard_copy = {}

    def send_shard(k):
        cols = pl.ds(FROM[k], WIDE[k])
        shard_copy[k] = send(pack.at[1 - c, :, cols], both.at[c, :, cols], twin)
        both[c, :, FROM[k] : FROM[k] + WIDE[k]] = pack[c, :, FROM[k] : FROM[k] + WIDE[k]]

    send_shard(0)
    send_shard(1)
    half_rows = pl.ds(pl.multiple_of(part * OWN, OWN), OWN)
    landing = src2.at[pl.ds(pl.multiple_of((1 - c) * BLOCK + part * OWN, OWN), OWN)]
    landed = src2.at[pl.ds(pl.multiple_of(c * BLOCK + part * OWN, OWN), OWN)]
    src_copy = send(src_in.at[half_rows], landing, ahead)
    tgt_copy = send(tgt_in, tgt2.at[my_block], twin)
    d_out_copy = send(d_out.at[their_rows], dgot.at[c], twin)
    gather0(0)
    gather0(1)
    pack_feed(0)
    send_shard(2)
    pack_attention(2)
    send_shard(3)
    pack_feed(1)
    send_shard(4)
    tgt2[my_block, :] = tgt_in[...]
    dgot[c] = d_out[my_rows, :]
    side[...] = jnp.zeros((2, 16, D), F32)
    gather1(0)
    gather0(2)
    gather1(1)
    gather2(0)
    gather1(2)
    gather2(1)
    src_copy.wait_recv()
    src_half = send(landed, landed, beside)
    gather3(0)
    gather0(3)
    gather3(1)
    gather2(2)
    gather0(4)
    src_half.wait_recv()
    src_share = send(src2.at[my_block], src2.at[my_block], twin)

    gather4(0)
    unpack_vectors()
    src_share.wait_recv()
    sum0(0, 0, attend(0, 0, src2, src2))
    sum0(0, 1, attend(0, 1, src2, src2))
    sum1(0, 0)
    sum1(0, 1)
    gather1(3)
    gather1(4)
    gather2(3)
    gather4(1)
    tgt_copy.wait_recv()
    sum0(1, 0, attend(1, 0, tgt2, tgt2))
    norm(0, 0, 0, src2, h0, "h0")
    sum0(1, 1, attend(1, 1, tgt2, tgt2))
    sum1(1, 0)
    norm(0, 0, 1, src2, h0, "h0")
    sum1(1, 1)
    gather3(2)
    gather2(4)
    norm(1, 2, 0, tgt2, h2, "h2")
    norm(1, 2, 1, tgt2, h2, "h2")
    gather3(3)
    gather4(2)
    share_wait("h0", 0)
    sum0(2, 0, feed(0, 0, h0))
    share_wait("h0", 1)
    sum0(2, 1, feed(0, 1, h0))
    sum1(2, 0)
    sum1(2, 1)
    feed_slope(0, 0)
    feed_slope(0, 1)
    gather3(4)
    gather4(3)
    share_wait("h2", 0)
    share_wait("h2", 1)
    norm(2, 1, 0, h0, enc, "enc")
    share_wait("enc", 0)
    sum0(3, 0, attend(2, 0, h2, enc))
    norm(2, 1, 1, h0, enc, "enc")
    sum1(3, 0)
    share_wait("enc", 1)
    sum0(3, 1, attend(2, 1, h2, enc))
    sum1(3, 1)
    gather4(4)
    norm(3, 3, 0, h2, h3, "h3")
    share_wait("h3", 0)
    sum0(4, 0, feed(1, 0, h3))
    norm(3, 3, 1, h2, h3, "h3")
    sum1(4, 0)
    share_wait("h3", 1)
    sum0(4, 1, feed(1, 1, h3))
    sum1(4, 1)
    feed_slope(1, 0)
    feed_slope(1, 1)
    d_out_copy.wait_recv()

    def cotangent(b, rows):
        return dgot[b, rows, :].astype(F32)

    def rounded(n, i):
        def top(b, rows):
            return (gres[n][b, rows, :] + summed(i, b, rows)).astype(LOW).astype(F32)

        return top

    def from_cross(b, rows):
        return summed(6, b, rows).astype(LOW).astype(F32)

    norm(4, 4, 0, h3, dec_snd, None)
    norm_back(4, 0, cotangent)
    share_wait(("gl", 4), 0)
    sum0(5, 0, feed_back(1, 4, 0))
    norm(4, 4, 1, h3, dec_snd, None)
    norm_back(4, 1, cotangent)
    sum1(5, 0)
    share_wait(("gl", 4), 1)
    feed_down_weights(1, 4)
    scatter0(4, 1)
    sum0(5, 1, feed_back(1, 4, 1))
    sum1(5, 1)
    feed_up_weights(1, h3)
    scatter0(4, 0)
    dec_copy = send(dec_snd.at[1 - c], tokens.at[0, my_rows], twin)
    tokens[0, my_rows, :] = dec_snd[c]
    sum2(5, 0)
    norm_back(3, 0, rounded(4, 5))
    share_wait(("gl", 3), 0)
    cross_back(0)
    sum2(5, 1)
    norm_back(3, 1, rounded(4, 5))
    sum1(6, 0)
    share_wait(("gl", 3), 1)
    cross_back(1)
    sum1(6, 1)
    sum1(7, 0)
    sum1(7, 1)
    scatter1(4)
    attend_weights(2, h2, enc)
    attend_weights_out(2, 3, enc)
    scatter0(3)
    sum2(6, 0)
    norm_back(1, 0, from_cross)
    share_wait(("gl", 1), 0)
    sum0(8, 0, feed_back(0, 1, 0))
    sum2(6, 1)
    norm_back(1, 1, from_cross)
    sum1(8, 0)
    share_wait(("gl", 1), 1)
    sum0(8, 1, feed_back(0, 1, 1))
    sum1(8, 1)
    feed_up_weights(0, h0)
    feed_down_weights(0, 1)
    scatter0(2)
    scatter2(4)
    sum2(7, 0)
    norm_back(2, 0, rounded(3, 7))
    sum2(7, 1)
    norm_back(2, 1, rounded(3, 7))
    scatter1(3)
    share_wait(("gl", 2), 0)
    self_back(1, 2, 0, 9)
    sum2(8, 0)
    norm_back(0, 0, rounded(1, 8))
    share_wait(("gl", 2), 1)
    self_back(1, 2, 1, 9)
    sum2(8, 1)
    norm_back(0, 1, rounded(1, 8))
    sum1(9, 0)
    sum1(9, 1)
    scatter3(4)
    scatter1(2)
    attend_weights(1, tgt2, tgt2)
    attend_weights_out(1, 2, tgt2)
    scatter0(1)
    share_wait(("gl", 0), 0)
    self_back(0, 0, 0, 10)
    share_wait(("gl", 0), 1)
    self_back(0, 0, 1, 10)
    attend_weights(0, src2, src2)
    attend_weights_out(0, 0, src2)
    for a in range(3):
        bias_sums(a)
    for f in range(2):
        up_sums(f)
    pack_vector_grads()
    scatter0(0)
    sum1(10, 0)
    sum1(10, 1)
    scatter2(3)
    scatter1(1)
    scatter4(4)
    scatter1(0)
    scatter3(3)
    scatter2(2)
    scatter2(1)
    scatter4(3)
    for b in range(2):
        sum2(9, b)
        tgt_snd[b] = (gres[2][b] + summed(9, b, slice(None))).astype(LOW)
    tgt_back = send(tgt_snd.at[1 - c], tokens.at[2, my_rows], twin)
    tokens[2, my_rows, :] = tgt_snd[c]
    piece_rows = pl.ds(pl.multiple_of(part * STEP, STEP), STEP)
    their_piece = pl.ds(pl.multiple_of(mine + part * STEP, STEP), STEP)
    for b in range(2):
        sum2(10, b)
        src_snd[b] = (gres[0][b] + summed(10, b, slice(None))).astype(LOW)
    src_back = send(src_snd.at[c, piece_rows], grad_src.at[their_piece], behind)
    src_back2 = send(src_snd.at[1 - c, piece_rows], grad_src.at[their_piece], twin_behind)
    scatter3(2)
    scatter2(0)
    scatter3(1)
    scatter4(2)
    scatter3(0)
    src_back.wait_recv()
    src_back2.wait_recv()
    near = grad_src.at[pl.ds(pl.multiple_of(part * STEP, STEP), STEP)]
    far = grad_src.at[pl.ds(pl.multiple_of(part * STEP + OWN, STEP), STEP)]
    src_last = (send(near, near, beside), send(far, far, beside))
    scatter5(4)
    scatter4(1)
    scatter5(3)
    scatter4(0)
    scatter5(2)
    scatter5(1)
    scatter5(0)
    for k in (4, 3, 2, 1, 0):
        scatter6(k)
    for copy in (dec_copy, tgt_back) + src_last:
        copy.wait_recv()
    tokens[1] = grad_src[...]
    for copy in started:
        copy.wait_send()


def run_layers(*operands):
    def low(*shape):
        return pltpu.VMEM(shape, LOW)

    def wide(*shape):
        return pltpu.VMEM(shape, F32)

    half = [max(CUT[n][1], n - CUT[n][1]) for n in WIDE]
    quarter = [384 if n == 1536 else 256 for n in WIDE]
    scratch = [low(4, 4, CHIP, n) for n in WIDE] * 2
    scratch += [low(4, 2, CHIP, n) for n in half]
    scratch += [low(4, 4, CHIP, n) for n in half]
    scratch += [low(4, CHIP, n) for n in quarter]
    scratch += [low(4, CHIP, n) for n in half]
    scratch += [low(CHIP, n) for n in WIDE] * 2
    scratch += [wide(CHIP, n) for n in WIDE]
    scratch += [low(2, BLOCK, D)] * N_SUM + [low(2, OWN, D)] * (3 * N_SUM)
    scratch += [wide(2, BLOCK, D)] * 4
    scratch += [low(2, 32, ALL)] * 2 + [low(ROWS, D)] * 6 + [low(2, OWN, D)]
    scratch += [low(2, OWN, D)] * 3 + [low(BLOCK, D)]
    scratch += [low(ROWS, D)] * 5 + [wide(2, OWN, D)] * 10 + [wide(2, OWN, 1)] * 5
    scratch += [low(ROWS, 640)] * 3 + [wide(6, BLOCK, BLOCK)] * 3 + [low(ROWS, 256)] * 3
    scratch += [low(ROWS, 640)] * 3 + [wide(8, 640)] * 3
    scratch += [wide(ROWS, D)] * 2 + [low(ROWS, D)] * 4 + [wide(8, D)] * 4
    scratch += [wide(16, D), wide(2, 16, D), wide(8, 640), wide(128, 128)]
    scratch += [pltpu.SemaphoreType.DMA((N_SEM,))] * 2
    vmem = pl.BlockSpec(memory_space=pltpu.VMEM)
    shapes = [
        jax.ShapeDtypeStruct((3, BLOCK, D), LOW),
        jax.ShapeDtypeStruct((2, PIECE, ALL), F32),
    ]
    return pl.pallas_call(
        layers,
        out_shape=shapes,
        in_specs=[vmem] * len(operands),
        out_specs=[vmem] * len(shapes),
        scratch_shapes=scratch,
        compiler_params=pltpu.CompilerParams(
            collective_id=0, has_side_effects=True, vmem_limit_bytes=62 * 2**20
        ),
    )(*operands)


def selector():
    table = np.zeros((D, 128), np.float32)
    for chip in range(16):
        for i, row in enumerate((0, 1, 24, 25)):
            table[CHIP * chip + row, 4 * chip + i] = 1.0
    return table


def place_results(tokens_in, grads_in, *refs):
    outs, (tokens, grads, sem) = refs[:11], refs[11:]
    moves = [
        pltpu.make_async_copy(tokens_in, tokens, sem.at[0]),
        pltpu.make_async_copy(grads_in, grads, sem.at[1]),
    ]
    for move in moves:
        move.start()
    attn_in, attn_out, w_up, w_down, qv, up, gains, shifts = outs[3:]
    moves[0].wait()
    for i, out in enumerate(outs[:3]):
        out[...] = tokens[i].astype(out.dtype)
    moves[1].wait()
    for a in range(3):
        for m in range(4):
            col = FROM[ATT_CHUNK[a]] + m * 192
            joined = jnp.concatenate([grads[h, :, col : col + 192] for h in range(2)], axis=1)
            if m < 3:
                attn_in[a, m] = joined
            else:
                attn_out[a] = joined
    for f in range(2):
        col = FROM[FFN_CHUNK[f]]
        for half in range(2):
            w_up[f, :, half * D : (half + 1) * D] = grads[half, :, col : col + D]
            w_down[f, :, half * D : (half + 1) * D] = grads[half, :, col + D : col + 2 * D]
    across = (grads[0, :, D:896] + grads[1, :, D:896]).T
    gains[...] = across[:5]
    shifts[...] = across[5:15]
    for a in range(3):
        for i in range(2):
            col = D + VEC_QV + 6 * a + 3 * i
            qv[a, i] = jnp.concatenate([grads[h, 0:2, col : col + 3] for h in range(2)], axis=1)
    for f in range(2):
        col = D + VEC_UP + 12 * f
        up[f] = jnp.concatenate([grads[h, 0:2, col : col + 12] for h in range(2)], axis=1)


def placed_results(*results):
    vmem = pl.BlockSpec(memory_space=pltpu.VMEM)
    shapes = [
        jax.ShapeDtypeStruct((BLOCK, D), LOW),
        jax.ShapeDtypeStruct((BLOCK, D), F32),
        jax.ShapeDtypeStruct((BLOCK, D), F32),
        jax.ShapeDtypeStruct((3, 3, PIECE, 384), F32),
        jax.ShapeDtypeStruct((3, PIECE, 384), F32),
        jax.ShapeDtypeStruct((2, PIECE, 1536), F32),
        jax.ShapeDtypeStruct((2, PIECE, 1536), F32),
        jax.ShapeDtypeStruct((3, 2, 2, 6), F32),
        jax.ShapeDtypeStruct((2, 2, 24), F32),
        jax.ShapeDtypeStruct((5, PIECE), F32),
        jax.ShapeDtypeStruct((10, PIECE), F32),
    ]
    return pl.pallas_call(
        place_results,
        out_shape=shapes,
        in_specs=[pl.BlockSpec(memory_space=pltpu.HBM)] * len(results),
        out_specs=[vmem] * len(shapes),
        scratch_shapes=[pltpu.VMEM(r.shape, r.dtype) for r in results]
        + [pltpu.SemaphoreType.DMA((len(results),))],
        compiler_params=pltpu.CompilerParams(vmem_limit_bytes=32 * 2**20),
    )(*results)


def local(
    src_in,
    tgt_in,
    src_seg,
    tgt_seg,
    attn_in,
    attn_out,
    w_up,
    w_down,
    qv_bias,
    up_bias,
    gains,
    shifts,
    d_out,
):
    pick = jnp.asarray(selector(), LOW)
    results = run_layers(
        attn_in,
        attn_out.transpose(0, 2, 1),
        w_up,
        w_down.transpose(0, 2, 1),
        qv_bias.transpose(0, 1, 3, 2),
        up_bias.transpose(0, 2, 1),
        gains,
        shifts,
        src_in,
        tgt_in,
        d_out,
        src_seg.reshape(64, 128),
        tgt_seg.reshape(64, 128),
        pick,
    )
    dec, src, tgt, att_in, att_out, up, down, qv, up_vec, gain, shift = placed_results(*results)
    return (
        dec,
        src,
        tgt,
        att_in,
        att_out.transpose(0, 2, 1),
        up,
        down.transpose(0, 2, 1),
        qv.transpose(0, 1, 3, 2),
        up_vec.transpose(0, 2, 1),
        gain,
        shift,
    )


def solution(mesh):
    placed = (
        P(("section", "dp"), None),
        P(("section", "dp"), None),
        P(),
        P(),
        P(None, None, "section", "tensor"),
        P(None, "tensor", "section"),
        P(None, "section", "tensor"),
        P(None, "tensor", "section"),
        P(None, None, "tensor", "section"),
        P(None, "tensor", "section"),
        P(None, "section"),
        P(None, "section"),
        P(("section", "dp"), None),
    )
    return jax.shard_map(
        local,
        mesh=mesh,
        in_specs=placed,
        out_specs=(placed[0], placed[0], placed[0]) + placed[4:12],
        check_vma=False,
    )
```

```python
import jax
import jax.numpy as jnp
import numpy as np
from jax import lax
from jax.experimental import pallas as pl
from jax.experimental.pallas import tpu as pltpu
from jax.sharding import PartitionSpec as P

LOW = jnp.bfloat16
F32 = jnp.float32
MESH = pl.DeviceIdType.MESH
D = 768
HEAD = 64
BLOCK = 128
OWN = 64
ROWS = 2 * BLOCK
PIECE = 24
CHIP = 48
HEADS = 3
STEP = 32

WIDE = (896, 768, 1536, 768, 1536)
FROM = (0, 896, 1664, 3200, 3968)
ALL = 5504
CUT = {896: (256, 384, 640), 768: (256, 384, 640), 1536: (384, 768, 1152)}
ATT_CHUNK = (0, 1, 3)
FFN_CHUNK = (2, 4)
VEC_QV = 16
VEC_UP = 34
OUT_ROW = (10, 13, 11, 12, 14)
N_SUM = 11
N_SEM = 260


def nn(left, right):
    return jnp.dot(left, right, preferred_element_type=F32)


def nt(left, right):
    return lax.dot_general(left, right, (((1,), (1,)), ((), ())), preferred_element_type=F32)


def tn(left, right):
    return lax.dot_general(left, right, (((0,), (0,)), ((), ())), preferred_element_type=F32)


def normal_part(value):
    return 0.5 * (1.0 + lax.erf(value * 0.7071067811865476))


def layers(*refs):
    refs = list(refs)

    def take(count):
        part, refs[:] = refs[:count], refs[count:]
        return part

    attn_in, attn_out, w_up, w_down, qv_bias, up_bias, gains, shifts = take(8)
    src_in, tgt_in, d_out, src_seg, tgt_seg, pick = take(6)
    tokens, grads = take(2)
    w, g, r1, r2, q1, q2, dsnd, drcv, tot = [take(5) for _ in range(9)]
    snd1, rcv1, snd2, rcv2 = [take(N_SUM) for _ in range(4)]
    own = take(4)
    pack, both, src2, tgt2, h0, enc, h2, h3, dgot, dec_snd, tgt_snd, src_snd, grad_src = take(13)
    gl, gres, hat, rstd = [take(5) for _ in range(4)]
    qkv, prob, ctx, dqkv, bias = [take(3) for _ in range(5)]
    pre, act, dpre, up_row, up_sum = [take(2) for _ in range(5)]
    vec, side, bias_sum, flat = take(4)
    send_sem, recv_sem = take(2)

    me = lax.axis_index("section")
    z, y, c = me // 8, lax.rem(me // 2, 4), lax.rem(me, 2)
    chip = me // 2
    replica = lax.axis_index("dp")
    zp, zm, z2 = lax.rem(z + 1, 4), lax.rem(z + 3, 4), lax.rem(z + 2, 4)
    yp, ym, y2 = lax.rem(y + 1, 4), lax.rem(y + 3, 4), lax.rem(y + 2, 4)

    def at(zz, yy):
        return {"section": zz * 8 + yy * 2 + c}

    dzp, dzm, dyp, dym = at(zp, y), at(zm, y), at(z, yp), at(z, ym)
    twin = {"section": me + 1 - 2 * c}
    beside = {"tensor": 1 - lax.axis_index("tensor")}
    partner = {"dp": 1 - replica}
    behind = {"section": lax.rem(me + 29, 32)}
    ahead = {"section": lax.rem(me + 3, 32)}
    twin_behind = {"section": lax.rem(me + 1 - 2 * c + 29, 32)}
    other_ahead = {"section": lax.rem(me + 3, 32) + 2 * c - 1}
    my_block = pl.ds(pl.multiple_of(c * BLOCK, BLOCK), BLOCK)
    their_block = pl.ds(pl.multiple_of((1 - c) * BLOCK, BLOCK), BLOCK)
    mine = pl.multiple_of(c * OWN, OWN)
    theirs = pl.multiple_of((1 - c) * OWN, OWN)
    my_rows, their_rows = pl.ds(mine, OWN), pl.ds(theirs, OWN)
    part = lax.axis_index("tensor")

    barrier = pltpu.get_barrier_semaphore()
    greeted = (dzp, dzm, dyp, dym, twin, beside, partner)
    greeted += (behind, ahead, twin_behind, other_ahead)
    for device in greeted:
        pl.semaphore_signal(barrier, inc=1, device_id=device, device_id_type=MESH)

    def pack_attention(a):
        k = ATT_CHUNK[a]
        for half in range(2):
            cols = slice(half * 192, (half + 1) * 192)
            parts = [attn_in[a, m, :, cols] for m in range(3)] + [attn_out[a, :, cols]]
            pack[half, :PIECE, FROM[k] : FROM[k] + D] = jnp.concatenate(parts, axis=1)

    def pack_feed(f):
        k = FFN_CHUNK[f]
        for half in range(2):
            cols = slice(half * D, (half + 1) * D)
            pack[half, :PIECE, FROM[k] : FROM[k] + D] = w_up[f, :, cols]
            pack[half, :PIECE, FROM[k] + D : FROM[k] + 2 * D] = w_down[f, :, cols]

    def pack_vectors():
        across = jnp.concatenate([gains[...], shifts[...]], axis=0).astype(F32).T
        for half in range(2):
            pieces = [qv_bias[a, i, :, half * 3 : half * 3 + 3] for a in range(3) for i in range(2)]
            pieces += [up_bias[f, :, half * 12 : half * 12 + 12] for f in range(2)]
            along = jnp.concatenate([piece.astype(F32) for piece in pieces], axis=1)
            along = jnp.concatenate([along, jnp.zeros((PIECE - 2, 42), F32)], axis=0)
            blank = jnp.zeros((PIECE, 1), F32), jnp.zeros((PIECE, 70), F32)
            joined = jnp.concatenate([across, blank[0], along, blank[1]], axis=1)
            pack[half, :PIECE, D:896] = joined.astype(LOW)

    pack_attention(0)
    pack_vectors()
    pl.semaphore_wait(barrier, len(greeted))

    started = []

    def send(src, dst, device):
        index = len(started)
        copy = pltpu.make_async_remote_copy(
            src_ref=src,
            dst_ref=dst,
            send_sem=send_sem.at[index],
            recv_sem=recv_sem.at[index],
            device_id=device,
            device_id_type=MESH,
        )
        started.append(copy)
        copy.start()
        return copy

    def halves(k):
        a1, a2, b1 = CUT[WIDE[k]]
        n = WIDE[k]
        return (
            pl.ds(0, a2),
            pl.ds(a2, n - a2),
            pl.ds(0, a1),
            pl.ds(a1, a2 - a1),
            pl.ds(a2, b1 - a2),
            pl.ds(b1, n - b1),
        )

    lo, hi = pl.ds(0, 2), pl.ds(2, 2)
    first, second, third, fourth = {}, {}, {}, {}

    def gather0(k):
        a, b = halves(k)[:2]
        cols = slice(FROM[k], FROM[k] + WIDE[k])
        shard_copy[k].wait_recv()
        joined = jnp.concatenate(
            [both[0, :PIECE, cols].astype(F32), both[1, :PIECE, cols].astype(F32)], axis=0
        )
        w[k][z, y] = joined.astype(LOW)
        src_a, src_b = w[k].at[z, y, :, a], w[k].at[z, y, :, b]
        first[k] = [
            send(src_a, src_a, dzp),
            send(src_b, src_b, dyp),
            send(src_a, src_a, dzm),
            send(src_b, src_b, dym),
        ]

    def gather1(k):
        ap, am, bp, bm = halves(k)[2:]
        second[k] = []
        order = (
            (w[k].at[zm, y, :, ap], dzp),
            (w[k].at[z, ym, :, bp], dyp),
            (w[k].at[zp, y, :, am], dzm),
            (w[k].at[z, yp, :, bm], dym),
        )
        for copy, (block, device) in zip(first[k], order):
            copy.wait_recv()
            second[k].append(send(block, block, device))

    def gather2(k):
        a, b = halves(k)[:2]
        for copy in second[k]:
            copy.wait_recv()
        row, line = w[k].at[:, y, :, a], w[k].at[z, :, :, b]
        third[k] = [
            send(row, row, dyp),
            send(line, line, dzp),
            send(row, row, dym),
            send(line, line, dzm),
        ]

    def gather3(k):
        a, b = halves(k)[:2]
        fourth[k] = []
        order = (
            (w[k].at[lo, ym, :, a], dyp),
            (w[k].at[zm, lo, :, b], dzp),
            (w[k].at[hi, yp, :, a], dym),
            (w[k].at[zp, hi, :, b], dzm),
        )
        for copy, (block, device) in zip(third[k], order):
            copy.wait_recv()
            fourth[k].append(send(block, block, device))

    def gather4(k):
        for copy in fourth[k]:
            copy.wait_recv()

    def weight(k, start, stop):
        return w[k][:, :, :, start:stop].reshape(D, stop - start)

    down1, down2, down3, down4, down5, down6 = {}, {}, {}, {}, {}, {}

    def scatter0(k, half=None):
        a, b = halves(k)[:2]
        na, nb = pl.ds(0, a.size), pl.ds(0, b.size)
        copies = down1.setdefault(k, {})
        if half != 1:
            copies[0] = send(g[k].at[z2, lo, :, a], r1[k].at[0, :, :, na], dzp)
            copies[2] = send(g[k].at[z2, hi, :, a], r1[k].at[2, :, :, na], dzm)
        if half != 0:
            copies[1] = send(g[k].at[lo, y2, :, b], r1[k].at[1, :, :, nb], dyp)
            copies[3] = send(g[k].at[hi, y2, :, b], r1[k].at[3, :, :, nb], dym)

    def scatter1(k):
        a, b = halves(k)[:2]
        na, nb = pl.ds(0, a.size), pl.ds(0, b.size)
        copies, down2[k] = down1[k], []
        copies[0].wait_recv()
        g[k][zp, lo, :, a] += r1[k][0, :, :, na]
        down2[k].append(send(g[k].at[zp, :, :, a], r2[k].at[0, :, :, na], dzp))
        copies[1].wait_recv()
        g[k][lo, yp, :, b] += r1[k][1, :, :, nb]
        down2[k].append(send(g[k].at[:, yp, :, b], r2[k].at[1, :, :, nb], dyp))
        copies[2].wait_recv()
        g[k][zm, hi, :, a] += r1[k][2, :, :, na]
        down2[k].append(send(g[k].at[zm, :, :, a], r2[k].at[2, :, :, na], dzm))
        copies[3].wait_recv()
        g[k][hi, ym, :, b] += r1[k][3, :, :, nb]
        down2[k].append(send(g[k].at[:, ym, :, b], r2[k].at[3, :, :, nb], dym))

    def scatter2(k):
        a, b, ap, am, bp, bm = halves(k)
        na, nb = pl.ds(0, a.size), pl.ds(0, b.size)
        copies = down2[k]
        copies[0].wait_recv()
        copies[2].wait_recv()
        g[k][z, :, :, a] += r2[k][0, :, :, na] + r2[k][2, :, :, na]
        down3[k] = [
            send(g[k].at[z, y2, :, ap], q1[k].at[0, :, pl.ds(0, ap.size)], dyp),
            send(g[k].at[z, y2, :, am], q1[k].at[1, :, pl.ds(0, am.size)], dym),
        ]
        copies[1].wait_recv()
        copies[3].wait_recv()
        g[k][:, y, :, b] += r2[k][1, :, :, nb] + r2[k][3, :, :, nb]
        down3[k] += [
            send(g[k].at[z2, y, :, bp], q1[k].at[2, :, pl.ds(0, bp.size)], dzp),
            send(g[k].at[z2, y, :, bm], q1[k].at[3, :, pl.ds(0, bm.size)], dzm),
        ]

    def scatter3(k):
        a, b, ap, am, bp, bm = halves(k)
        na, nb = pl.ds(0, a.size), pl.ds(0, b.size)
        copies, down4[k] = down3[k], []
        copies[0].wait_recv()
        g[k][z, yp, :, ap] += q1[k][0, :, : ap.size]
        down4[k].append(send(g[k].at[z, yp, :, a], q2[k].at[0, :, na], dyp))
        copies[1].wait_recv()
        g[k][z, ym, :, am] += q1[k][1, :, : am.size]
        down4[k].append(send(g[k].at[z, ym, :, a], q2[k].at[1, :, na], dym))
        copies[2].wait_recv()
        g[k][zp, y, :, bp] += q1[k][2, :, : bp.size]
        down4[k].append(send(g[k].at[zp, y, :, b], q2[k].at[2, :, nb], dzp))
        copies[3].wait_recv()
        g[k][zm, y, :, bm] += q1[k][3, :, : bm.size]
        down4[k].append(send(g[k].at[zm, y, :, b], q2[k].at[3, :, nb], dzm))

    def scatter4(k):
        a, b = halves(k)[:2]
        for copy in down4[k]:
            copy.wait_recv()
        for cols, i in ((a, 0), (b, 2)):
            n = pl.ds(0, cols.size)
            got = q2[k][i, :, n].astype(F32) + q2[k][i + 1, :, n].astype(F32)
            dsnd[k][:, cols] = (g[k][z, y, :, cols].astype(F32) + got).astype(LOW)
        down5[k] = send(dsnd[k], drcv[k], partner)

    def scatter5(k):
        down5[k].wait_recv()
        tot[k][...] = dsnd[k][...].astype(F32) + drcv[k][...].astype(F32)
        rows_mine = pl.ds(pl.multiple_of(c * PIECE, PIECE), PIECE)
        rows_theirs = pl.ds(pl.multiple_of((1 - c) * PIECE, PIECE), PIECE)
        cols = pl.ds(FROM[k], WIDE[k])
        down6[k] = send(tot[k].at[rows_theirs], grads.at[c, :, cols], twin)
        grads[c, :, cols] = tot[k][rows_mine, :]

    def scatter6(k):
        down6[k].wait_recv()

    def put_grad(k, start, value):
        n = value.shape[1]
        g[k][:, :, :, start : start + n] = value.astype(LOW).reshape(4, 4, CHIP, n)

    hop1, hop2 = {}, {}

    def sum0(i, b, part):
        own[i % 4][b] = part
        snd1[i][b] = part.astype(LOW)
        hop1[i, b] = send(snd1[i].at[b, their_rows], rcv1[i].at[b], twin)

    def sum1(i, b):
        hop1[i, b].wait_recv()
        snd2[i][b] = (own[i % 4][b, my_rows, :] + rcv1[i][b].astype(F32)).astype(LOW)
        hop2[i, b] = send(snd2[i].at[b], rcv2[i].at[b], beside)

    def sum2(i, b):
        hop2[i, b].wait_recv()

    def summed(i, b, rows):
        return snd2[i][b, rows, :].astype(F32) + rcv2[i][b, rows, :].astype(F32)

    shared = {}

    def share(name, ref, b):
        view = ref.at[pl.ds(pl.multiple_of(b * BLOCK + mine, OWN), OWN)]
        shared[name, b] = send(view, view, twin)

    def share_wait(name, b):
        shared[name, b].wait_recv()

    def norm(i, n, b, x_ref, out_ref, name):
        sum2(i, b)
        gain, shift, out_shift = (vec[r : r + 1, :] for r in (n, 5 + n, OUT_ROW[n]))
        for r in range(0, OWN, STEP):
            rows = pl.ds(r, STEP)
            place = pl.ds(pl.multiple_of(b * BLOCK + mine + r, STEP), STEP)
            resid = x_ref[place, :].astype(F32) + (summed(i, b, rows) + out_shift)
            center = resid - jnp.mean(resid, axis=1, keepdims=True)
            spread = jnp.mean(center * center, axis=1, keepdims=True)
            scale = lax.rsqrt(spread + 1e-05)
            hat[n][b, rows, :] = center * scale
            rstd[n][b, rows, :] = scale
            result = (center * scale * gain + shift).astype(LOW)
            if name is None:
                out_ref[b, rows, :] = result
            else:
                out_ref[place, :] = result
        if name is not None:
            share(name, out_ref, b)

    def norm_back(n, b, top):
        gain = vec[n : n + 1, :]
        sums = [jnp.zeros((8, D), F32) for _ in range(3)]
        for r in range(0, OWN, STEP):
            rows = pl.ds(r, STEP)
            place = pl.ds(pl.multiple_of(b * BLOCK + mine + r, STEP), STEP)
            grad = top(b, rows)
            x_hat = hat[n][b, rows, :]
            d_hat = grad * gain
            mean1 = jnp.mean(d_hat, axis=1, keepdims=True)
            mean2 = jnp.mean(d_hat * x_hat, axis=1, keepdims=True)
            resid = rstd[n][b, rows, :] * (d_hat - mean1 - x_hat * mean2)
            gres[n][b, rows, :] = resid
            gl[n][place, :] = resid.astype(LOW)
            for j, value in enumerate((grad * x_hat, grad, resid)):
                sums[j] = sums[j] + jnp.sum(value.reshape(STEP // 8, 8, D), axis=0)
        share(("gl", n), gl[n], b)
        for row, value in zip((n, 5 + n, OUT_ROW[n]), sums):
            side[b, row : row + 1, :] = jnp.sum(value, axis=0, keepdims=True)

    def lanes(start, width):
        return lax.broadcasted_iota(jnp.int32, (1, width), 1) + start

    def segment_row(table, shift, half):
        section = lax.rem(2 * chip + half + shift, 32)
        row = table[pl.ds(2 * section + replica, 1), :].astype(F32)
        return jnp.broadcast_to(row, (BLOCK, BLOCK))

    def allowed(a, half):
        query = segment_row(src_seg, 29, half) if a == 0 else segment_row(tgt_seg, 0, half)
        keys = segment_row(tgt_seg, 0, half) if a == 1 else segment_row(src_seg, 29, half)
        allow = query.T == keys
        if a == 1:
            row = lax.broadcasted_iota(jnp.int32, (BLOCK, BLOCK), 0)
            col = lax.broadcasted_iota(jnp.int32, (BLOCK, BLOCK), 1)
            allow = allow & (row >= col)
        return allow

    def heads_of(a, rows, head):
        return (qkv[a][rows, s + head * HEAD : s + (head + 1) * HEAD] for s in (0, 192, 384))

    def block(b):
        return slice(b * BLOCK, (b + 1) * BLOCK)

    def attend(a, b, x_ref, y_ref):
        k = ATT_CHUNK[a]
        rows = block(b)
        scale = jnp.where(lanes(0, 640) < 192, 0.125, 1.0)
        row_bias = bias[a][0:1, :]
        if a < 2:
            joined = nn(x_ref[rows, :], weight(k, 0, 640))
        else:
            left = nn(x_ref[rows, :], weight(k, 0, 256))
            right = nn(y_ref[rows, :], weight(k, 128, 640))
            middle = jnp.where(lanes(128, 128) < 192, left[:, 128:], right[:, :128])
            joined = jnp.concatenate([left[:, :128], middle, right[:, 128:]], axis=1)
        qkv[a][rows, :] = ((joined + row_bias) * scale).astype(LOW)
        allow = allowed(a, b)
        parts = [jnp.zeros((BLOCK, HEAD), LOW)]
        for head in range(HEADS):
            q, key, v = heads_of(a, rows, head)
            score = jnp.where(allow, nt(q, key), -1e30)
            expo = jnp.exp(score - jnp.max(score, axis=1, keepdims=True))
            p = expo / jnp.sum(expo, axis=1, keepdims=True)
            prob[a][b * HEADS + head] = p
            parts.append(nn(p.astype(LOW), v).astype(LOW))
        joined = jnp.concatenate(parts, axis=1)
        ctx[a][rows, :] = joined
        return nt(joined, weight(k, 512, 768))

    def attend_back(a, n, b):
        k = ATT_CHUNK[a]
        rows = block(b)
        d_ctx = nn(gl[n][rows, :], weight(k, 512, 768)).astype(LOW)
        d_q, d_k, d_v = [], [], []
        for head in range(HEADS):
            q, key, v = heads_of(a, rows, head)
            d_c = d_ctx[:, HEAD * (head + 1) : HEAD * (head + 2)]
            p = prob[a][b * HEADS + head]
            d_p = nt(d_c, v)
            delta = jnp.sum(p * d_p, axis=1, keepdims=True)
            d_s = (p * (d_p - delta)).astype(LOW)
            d_q.append((nn(d_s, key).astype(LOW).astype(F32) * 0.125).astype(LOW))
            d_k.append(tn(d_s, q).astype(LOW))
            d_v.append(tn(p.astype(LOW), d_c).astype(LOW))
        blank = jnp.zeros((BLOCK, HEAD), LOW)
        joined = jnp.concatenate(d_q + d_k + d_v + [blank], axis=1)
        dqkv[a][rows, :] = joined
        return joined

    def bias_sums(a):
        total = jnp.sum(dqkv[a][...].astype(F32).reshape(ROWS // 8, 8, 640), axis=0)
        bias_sum[a : a + 1, :] = jnp.sum(total, axis=0, keepdims=True)

    def query_part(value):
        return jnp.where(lanes(0, 256) < 192, value.astype(F32), 0.0).astype(LOW)

    def key_part(value, start):
        return jnp.where(lanes(start, value.shape[1]) < 192, 0.0, value.astype(F32)).astype(LOW)

    def self_back(a, n, b, i):
        sum0(i, b, nt(attend_back(a, n, b), weight(ATT_CHUNK[a], 0, 640)))

    def cross_back(b):
        joined = attend_back(2, 3, b)
        sum0(6, b, nt(key_part(joined[:, 128:], 128), weight(3, 128, 640)))
        sum0(7, b, nt(query_part(joined[:, :256]), weight(3, 0, 256)))

    def attend_weights(a, x_ref, y_ref):
        k = ATT_CHUNK[a]
        if a < 2:
            put_grad(k, 0, tn(x_ref[...], dqkv[a][:, 0:512]))
        else:
            left = tn(x_ref[...], query_part(dqkv[a][:, 0:256]))
            put_grad(k, 0, left + tn(y_ref[...], key_part(dqkv[a][:, 0:256], 0)))
            put_grad(k, 256, tn(y_ref[...], dqkv[a][:, 256:512]))

    def attend_weights_out(a, n, y_ref):
        k = ATT_CHUNK[a]
        tail = jnp.concatenate([dqkv[a][:, 512:640], jnp.zeros((ROWS, 128), LOW)], axis=1)
        put_grad(k, 512, tn(y_ref[...], tail) + tn(gl[n][...], ctx[a][...]))

    def feed(f, b, x_ref):
        k = FFN_CHUNK[f]
        pre[f][block(b), :] = nn(x_ref[block(b), :], weight(k, 0, D)) + up_row[f][0:1, :]

        @pl.loop(0, BLOCK // 16)
        def _(step):
            rows = pl.ds(pl.multiple_of(b * BLOCK + step * 16, 16), 16)
            value = pre[f][rows, :]
            act[f][rows, :] = (value * normal_part(value)).astype(LOW)

        return nt(act[f][block(b), :], weight(k, D, 2 * D))

    def feed_slope(f, b):
        @pl.loop(0, BLOCK // 16)
        def _(step):
            rows = pl.ds(pl.multiple_of(b * BLOCK + step * 16, 16), 16)
            value = pre[f][rows, :]
            bell = jnp.exp(-0.5 * value * value) * 0.3989422804014327
            pre[f][rows, :] = normal_part(value) + value * bell

    def feed_back(f, n, b):
        k = FFN_CHUNK[f]
        d_act = nn(gl[n][block(b), :], weight(k, D, 2 * D))
        d_pre = (pre[f][block(b), :] * d_act).astype(LOW)
        dpre[f][block(b), :] = d_pre
        return nt(d_pre, weight(k, 0, D))

    def feed_up_weights(f, x_ref):
        put_grad(FFN_CHUNK[f], 0, tn(x_ref[...], dpre[f][...]))

    def up_sums(f):
        total = jnp.sum(dpre[f][...].astype(F32).reshape(ROWS // 8, 8, D), axis=0)
        up_sum[f][0:1, :] = jnp.sum(total, axis=0, keepdims=True)

    def feed_down_weights(f, n):
        put_grad(FFN_CHUNK[f], D, tn(gl[n][...], act[f][...]))

    def unpack_vectors():
        packed = weight(0, D, 896)
        vec[...] = packed.astype(F32).T[:16, :]
        flat[...] = tn(packed, pick[...])
        for a in range(3):
            r = VEC_QV + 6 * a
            zero = jnp.zeros((1, HEAD), F32)
            pieces = [flat[r + i : r + i + 1, :HEAD] for i in range(6)]
            row = jnp.concatenate(pieces[:3] + [zero] * 3 + pieces[3:] + [zero], axis=1)
            bias[a][0:1, :] = row
        for f in range(2):
            r = VEC_UP + 12 * f
            pieces = [flat[r + i : r + i + 1, :HEAD] for i in range(12)]
            up_row[f][0:1, :] = jnp.concatenate(pieces, axis=1)

    def pack_vector_grads():
        rows = []
        for a in range(3):
            for s in (0, 384):
                rows += [bias_sum[a : a + 1, s + i * HEAD : s + (i + 1) * HEAD] for i in range(3)]
        for f in range(2):
            rows += [up_sum[f][0:1, i * HEAD : (i + 1) * HEAD] for i in range(12)]
        rows.append(jnp.zeros((6, HEAD), F32))
        small = jnp.concatenate(rows, axis=0).astype(LOW)
        spread = nt(small, pick[:, :HEAD])
        table = jnp.concatenate([side[0] + side[1], spread, jnp.zeros((64, D), F32)], axis=0)
        put_grad(0, D, table.T)

    shard_copy = {}

    def send_shard(k):
        cols = pl.ds(FROM[k], WIDE[k])
        shard_copy[k] = send(pack.at[1 - c, :, cols], both.at[c, :, cols], twin)
        both[c, :, FROM[k] : FROM[k] + WIDE[k]] = pack[c, :, FROM[k] : FROM[k] + WIDE[k]]

    send_shard(0)
    pack_attention(1)
    send_shard(1)
    half_rows = pl.ds(pl.multiple_of(part * OWN, OWN), OWN)
    landing = src2.at[pl.ds(pl.multiple_of((1 - c) * BLOCK + part * OWN, OWN), OWN)]
    landed = src2.at[pl.ds(pl.multiple_of(c * BLOCK + part * OWN, OWN), OWN)]
    src_copy = send(src_in.at[half_rows], landing, ahead)
    gather0(0)
    gather0(1)
    pack_feed(0)
    send_shard(2)
    pack_attention(2)
    send_shard(3)
    pack_feed(1)
    send_shard(4)
    gather1(0)
    gather0(2)
    gather1(1)
    tgt_copy = send(tgt_in, tgt2.at[my_block], twin)
    d_out_copy = send(d_out.at[their_rows], dgot.at[c], twin)
    tgt2[my_block, :] = tgt_in[...]
    dgot[c] = d_out[my_rows, :]
    side[...] = jnp.zeros((2, 16, D), F32)
    gather2(0)
    gather1(2)
    gather2(1)
    src_copy.wait_recv()
    src_half = send(landed, landed, beside)
    gather3(0)
    gather0(3)
    gather3(1)
    gather2(2)
    gather0(4)
    src_half.wait_recv()
    src_share = send(src2.at[my_block], src2.at[my_block], twin)

    gather4(0)
    unpack_vectors()
    src_share.wait_recv()
    sum0(0, 0, attend(0, 0, src2, src2))
    sum0(0, 1, attend(0, 1, src2, src2))
    sum1(0, 0)
    sum1(0, 1)
    gather1(3)
    gather1(4)
    gather2(3)
    gather4(1)
    tgt_copy.wait_recv()
    sum0(1, 0, attend(1, 0, tgt2, tgt2))
    norm(0, 0, 0, src2, h0, "h0")
    sum0(1, 1, attend(1, 1, tgt2, tgt2))
    sum1(1, 0)
    norm(0, 0, 1, src2, h0, "h0")
    sum1(1, 1)
    gather3(2)
    gather2(4)
    norm(1, 2, 0, tgt2, h2, "h2")
    norm(1, 2, 1, tgt2, h2, "h2")
    gather3(3)
    gather4(2)
    share_wait("h0", 0)
    sum0(2, 0, feed(0, 0, h0))
    share_wait("h0", 1)
    sum0(2, 1, feed(0, 1, h0))
    sum1(2, 0)
    sum1(2, 1)
    feed_slope(0, 0)
    feed_slope(0, 1)
    gather3(4)
    gather4(3)
    share_wait("h2", 0)
    share_wait("h2", 1)
    norm(2, 1, 0, h0, enc, "enc")
    share_wait("enc", 0)
    sum0(3, 0, attend(2, 0, h2, enc))
    norm(2, 1, 1, h0, enc, "enc")
    sum1(3, 0)
    share_wait("enc", 1)
    sum0(3, 1, attend(2, 1, h2, enc))
    sum1(3, 1)
    gather4(4)
    norm(3, 3, 0, h2, h3, "h3")
    share_wait("h3", 0)
    sum0(4, 0, feed(1, 0, h3))
    norm(3, 3, 1, h2, h3, "h3")
    sum1(4, 0)
    share_wait("h3", 1)
    sum0(4, 1, feed(1, 1, h3))
    sum1(4, 1)
    feed_slope(1, 0)
    feed_slope(1, 1)
    d_out_copy.wait_recv()

    def cotangent(b, rows):
        return dgot[b, rows, :].astype(F32)

    def rounded(n, i):
        def top(b, rows):
            return (gres[n][b, rows, :] + summed(i, b, rows)).astype(LOW).astype(F32)

        return top

    def from_cross(b, rows):
        return summed(6, b, rows).astype(LOW).astype(F32)

    norm(4, 4, 0, h3, dec_snd, None)
    norm_back(4, 0, cotangent)
    share_wait(("gl", 4), 0)
    sum0(5, 0, feed_back(1, 4, 0))
    norm(4, 4, 1, h3, dec_snd, None)
    norm_back(4, 1, cotangent)
    sum1(5, 0)
    share_wait(("gl", 4), 1)
    feed_down_weights(1, 4)
    scatter0(4, 1)
    sum0(5, 1, feed_back(1, 4, 1))
    sum1(5, 1)
    feed_up_weights(1, h3)
    scatter0(4, 0)
    dec_copy = send(dec_snd.at[1 - c], tokens.at[0, my_rows], twin)
    tokens[0, my_rows, :] = dec_snd[c]
    sum2(5, 0)
    norm_back(3, 0, rounded(4, 5))
    share_wait(("gl", 3), 0)
    cross_back(0)
    sum2(5, 1)
    norm_back(3, 1, rounded(4, 5))
    sum1(6, 0)
    share_wait(("gl", 3), 1)
    cross_back(1)
    sum1(6, 1)
    sum1(7, 0)
    sum1(7, 1)
    scatter1(4)
    attend_weights(2, h2, enc)
    attend_weights_out(2, 3, enc)
    scatter0(3)
    sum2(6, 0)
    norm_back(1, 0, from_cross)
    share_wait(("gl", 1), 0)
    sum0(8, 0, feed_back(0, 1, 0))
    sum2(6, 1)
    norm_back(1, 1, from_cross)
    sum1(8, 0)
    share_wait(("gl", 1), 1)
    sum0(8, 1, feed_back(0, 1, 1))
    sum1(8, 1)
    feed_up_weights(0, h0)
    scatter0(2, 0)
    feed_down_weights(0, 1)
    scatter0(2, 1)
    scatter2(4)
    sum2(7, 0)
    norm_back(2, 0, rounded(3, 7))
    sum2(7, 1)
    norm_back(2, 1, rounded(3, 7))
    scatter1(3)
    share_wait(("gl", 2), 0)
    self_back(1, 2, 0, 9)
    sum2(8, 0)
    norm_back(0, 0, rounded(1, 8))
    share_wait(("gl", 2), 1)
    self_back(1, 2, 1, 9)
    sum2(8, 1)
    norm_back(0, 1, rounded(1, 8))
    sum1(9, 0)
    sum1(9, 1)
    scatter3(4)
    scatter1(2)
    attend_weights(1, tgt2, tgt2)
    attend_weights_out(1, 2, tgt2)
    scatter0(1)
    share_wait(("gl", 0), 0)
    self_back(0, 0, 0, 10)
    share_wait(("gl", 0), 1)
    self_back(0, 0, 1, 10)
    attend_weights(0, src2, src2)
    attend_weights_out(0, 0, src2)
    for a in range(3):
        bias_sums(a)
    for f in range(2):
        up_sums(f)
    pack_vector_grads()
    scatter0(0)
    sum1(10, 0)
    sum1(10, 1)
    scatter2(3)
    scatter1(1)
    scatter4(4)
    scatter1(0)
    scatter3(3)
    scatter2(2)
    scatter2(1)
    scatter4(3)
    for b in range(2):
        sum2(9, b)
        tgt_snd[b] = (gres[2][b] + summed(9, b, slice(None))).astype(LOW)
    tgt_back = send(tgt_snd.at[1 - c], tokens.at[2, my_rows], twin)
    tokens[2, my_rows, :] = tgt_snd[c]
    piece_rows = pl.ds(pl.multiple_of(part * STEP, STEP), STEP)
    their_piece = pl.ds(pl.multiple_of(mine + part * STEP, STEP), STEP)
    for b in range(2):
        sum2(10, b)
        src_snd[b] = (gres[0][b] + summed(10, b, slice(None))).astype(LOW)
    src_back = send(src_snd.at[c, piece_rows], grad_src.at[their_piece], behind)
    src_back2 = send(src_snd.at[1 - c, piece_rows], grad_src.at[their_piece], twin_behind)
    scatter3(2)
    scatter2(0)
    scatter3(1)
    scatter4(2)
    scatter3(0)
    src_back.wait_recv()
    src_back2.wait_recv()
    near = grad_src.at[pl.ds(pl.multiple_of(part * STEP, STEP), STEP)]
    far = grad_src.at[pl.ds(pl.multiple_of(part * STEP + OWN, STEP), STEP)]
    src_last = (send(near, near, beside), send(far, far, beside))
    scatter5(4)
    scatter4(1)
    scatter5(3)
    scatter4(0)
    scatter5(2)
    scatter5(1)
    scatter5(0)
    for k in (4, 3, 2, 1, 0):
        scatter6(k)
    for copy in (dec_copy, tgt_back) + src_last:
        copy.wait_recv()
    tokens[1] = grad_src[...]
    for copy in started:
        copy.wait_send()


def run_layers(*operands):
    def low(*shape):
        return pltpu.VMEM(shape, LOW)

    def wide(*shape):
        return pltpu.VMEM(shape, F32)

    half = [max(CUT[n][1], n - CUT[n][1]) for n in WIDE]
    quarter = [384 if n == 1536 else 256 for n in WIDE]
    scratch = [low(4, 4, CHIP, n) for n in WIDE] * 2
    scratch += [low(4, 2, CHIP, n) for n in half]
    scratch += [low(4, 4, CHIP, n) for n in half]
    scratch += [low(4, CHIP, n) for n in quarter]
    scratch += [low(4, CHIP, n) for n in half]
    scratch += [low(CHIP, n) for n in WIDE] * 2
    scratch += [wide(CHIP, n) for n in WIDE]
    scratch += [low(2, BLOCK, D)] * N_SUM + [low(2, OWN, D)] * (3 * N_SUM)
    scratch += [wide(2, BLOCK, D)] * 4
    scratch += [low(2, 32, ALL)] * 2 + [low(ROWS, D)] * 6 + [low(2, OWN, D)]
    scratch += [low(2, OWN, D)] * 3 + [low(BLOCK, D)]
    scratch += [low(ROWS, D)] * 5 + [wide(2, OWN, D)] * 10 + [wide(2, OWN, 1)] * 5
    scratch += [low(ROWS, 640)] * 3 + [wide(6, BLOCK, BLOCK)] * 3 + [low(ROWS, 256)] * 3
    scratch += [low(ROWS, 640)] * 3 + [wide(8, 640)] * 3
    scratch += [wide(ROWS, D)] * 2 + [low(ROWS, D)] * 4 + [wide(8, D)] * 4
    scratch += [wide(16, D), wide(2, 16, D), wide(8, 640), wide(128, 128)]
    scratch += [pltpu.SemaphoreType.DMA((N_SEM,))] * 2
    vmem = pl.BlockSpec(memory_space=pltpu.VMEM)
    shapes = [
        jax.ShapeDtypeStruct((3, BLOCK, D), LOW),
        jax.ShapeDtypeStruct((2, PIECE, ALL), F32),
    ]
    return pl.pallas_call(
        layers,
        out_shape=shapes,
        in_specs=[vmem] * len(operands),
        out_specs=[vmem] * len(shapes),
        scratch_shapes=scratch,
        compiler_params=pltpu.CompilerParams(
            collective_id=0, has_side_effects=True, vmem_limit_bytes=62 * 2**20
        ),
    )(*operands)


def selector():
    table = np.zeros((D, 128), np.float32)
    for chip in range(16):
        for i, row in enumerate((0, 1, 24, 25)):
            table[CHIP * chip + row, 4 * chip + i] = 1.0
    return table


def place_results(tokens_in, grads_in, *refs):
    outs, (tokens, grads, sem) = refs[:11], refs[11:]
    moves = [
        pltpu.make_async_copy(tokens_in, tokens, sem.at[0]),
        pltpu.make_async_copy(grads_in, grads, sem.at[1]),
    ]
    for move in moves:
        move.start()
    attn_in, attn_out, w_up, w_down, qv, up, gains, shifts = outs[3:]
    moves[0].wait()
    for i, out in enumerate(outs[:3]):
        out[...] = tokens[i].astype(out.dtype)
    moves[1].wait()
    for a in range(3):
        for m in range(4):
            col = FROM[ATT_CHUNK[a]] + m * 192
            joined = jnp.concatenate([grads[h, :, col : col + 192] for h in range(2)], axis=1)
            if m < 3:
                attn_in[a, m] = joined
            else:
                attn_out[a] = joined
    for f in range(2):
        col = FROM[FFN_CHUNK[f]]
        for half in range(2):
            w_up[f, :, half * D : (half + 1) * D] = grads[half, :, col : col + D]
            w_down[f, :, half * D : (half + 1) * D] = grads[half, :, col + D : col + 2 * D]
    across = (grads[0, :, D:896] + grads[1, :, D:896]).T
    gains[...] = across[:5]
    shifts[...] = across[5:15]
    for a in range(3):
        for i in range(2):
            col = D + VEC_QV + 6 * a + 3 * i
            qv[a, i] = jnp.concatenate([grads[h, 0:2, col : col + 3] for h in range(2)], axis=1)
    for f in range(2):
        col = D + VEC_UP + 12 * f
        up[f] = jnp.concatenate([grads[h, 0:2, col : col + 12] for h in range(2)], axis=1)


def placed_results(*results):
    vmem = pl.BlockSpec(memory_space=pltpu.VMEM)
    shapes = [
        jax.ShapeDtypeStruct((BLOCK, D), LOW),
        jax.ShapeDtypeStruct((BLOCK, D), F32),
        jax.ShapeDtypeStruct((BLOCK, D), F32),
        jax.ShapeDtypeStruct((3, 3, PIECE, 384), F32),
        jax.ShapeDtypeStruct((3, PIECE, 384), F32),
        jax.ShapeDtypeStruct((2, PIECE, 1536), F32),
        jax.ShapeDtypeStruct((2, PIECE, 1536), F32),
        jax.ShapeDtypeStruct((3, 2, 2, 6), F32),
        jax.ShapeDtypeStruct((2, 2, 24), F32),
        jax.ShapeDtypeStruct((5, PIECE), F32),
        jax.ShapeDtypeStruct((10, PIECE), F32),
    ]
    return pl.pallas_call(
        place_results,
        out_shape=shapes,
        in_specs=[pl.BlockSpec(memory_space=pltpu.HBM)] * len(results),
        out_specs=[vmem] * len(shapes),
        scratch_shapes=[pltpu.VMEM(r.shape, r.dtype) for r in results]
        + [pltpu.SemaphoreType.DMA((len(results),))],
        compiler_params=pltpu.CompilerParams(vmem_limit_bytes=32 * 2**20),
    )(*results)


def local(
    src_in,
    tgt_in,
    src_seg,
    tgt_seg,
    attn_in,
    attn_out,
    w_up,
    w_down,
    qv_bias,
    up_bias,
    gains,
    shifts,
    d_out,
):
    pick = jnp.asarray(selector(), LOW)
    results = run_layers(
        attn_in,
        attn_out.transpose(0, 2, 1),
        w_up,
        w_down.transpose(0, 2, 1),
        qv_bias.transpose(0, 1, 3, 2),
        up_bias.transpose(0, 2, 1),
        gains,
        shifts,
        src_in,
        tgt_in,
        d_out,
        src_seg.reshape(64, 128),
        tgt_seg.reshape(64, 128),
        pick,
    )
    dec, src, tgt, att_in, att_out, up, down, qv, up_vec, gain, shift = placed_results(*results)
    return (
        dec,
        src,
        tgt,
        att_in,
        att_out.transpose(0, 2, 1),
        up,
        down.transpose(0, 2, 1),
        qv.transpose(0, 1, 3, 2),
        up_vec.transpose(0, 2, 1),
        gain,
        shift,
    )


def solution(mesh):
    placed = (
        P(("section", "dp"), None),
        P(("section", "dp"), None),
        P(),
        P(),
        P(None, None, "section", "tensor"),
        P(None, "tensor", "section"),
        P(None, "section", "tensor"),
        P(None, "tensor", "section"),
        P(None, None, "tensor", "section"),
        P(None, "tensor", "section"),
        P(None, "section"),
        P(None, "section"),
        P(("section", "dp"), None),
    )
    return jax.shard_map(
        local,
        mesh=mesh,
        in_specs=placed,
        out_specs=(placed[0], placed[0], placed[0]) + placed[4:12],
        check_vma=False,
    )
```
